512 devices in a mesh: ctx: 64 (over z, x, core), kvh: 8 (over y).
Axes of the slice: x: 4, y: 8, z: 8, core: 2. Of those that a mesh axis runs over, the one named last changes fastest.
Arguments:
- tokens: bfloat16 [2, 4, 8192], P(None, None, 'ctx'), may hold values from -6 to 6
- lengths: int32 [4], replicated, may hold values from 4096 to 16384, as said below
- attn_gain: bfloat16 [8192], P('ctx'), may hold values from 0.25 to 1.75
- ffn_gain: bfloat16 [8192], P('ctx'), may hold values from 0.25 to 1.75
- w_q: bfloat16 [8192, 8192], P('ctx', 'kvh'), may hold values from -5 to 5
- w_k: bfloat16 [8192, 1024], P('ctx', 'kvh'), may hold values from -0.25 to 0.25
- w_v: bfloat16 [8192, 1024], P('ctx', 'kvh'), may hold values from -0.25 to 0.25
- w_o: bfloat16 [8192, 8192], P('kvh', 'ctx'), may hold values from -0.0625 to 0.0625
- w_gate: bfloat16 [8192, 28672], P('ctx', 'kvh'), may hold values from -0.0625 to 0.0625
- w_up: bfloat16 [8192, 28672], P('ctx', 'kvh'), may hold values from -0.0625 to 0.0625
- w_down: bfloat16 [28672, 8192], P('kvh', 'ctx'), may hold values from -0.03125 to 0.03125
- k_cache: bfloat16 [4, 16384, 8, 128], P(None, 'ctx', 'kvh'), may hold values from -112 to 112
- v_cache: bfloat16 [4, 16384, 8, 128], P(None, 'ctx', 'kvh'), may hold values from -6 to 6
Outputs:
- attended: bfloat16 [2, 4, 8192], P(None, None, 'ctx')
- layer_out: bfloat16 [2, 4, 8192], P(None, None, 'ctx')
The draws below stay inside these ranges and needn't reach their ends.
Inputs may be any that keep to these rules, and one draw needn't show every extreme that they name: `lengths`: every length is at least 4096, and some request has exactly 16384.
All inputs are finite; a program needn't handle non-finite values.
Results may differ from the reference program's by a relative error of at most 0.015.
Values may be sent and summed in bfloat16 or wider, within the bound.
A program may use at most 64 MiB of HBM per device.

```python
import math
import jax
import jax.numpy as jnp
from jax import lax

D = 8192
H = 64
KVH = 8
HD = 128
FF = 28672
B = 4
L_MAX = 16384


def chosen_heads(key):
    return jax.random.randint(key, (KVH,), 0, H // KVH)


def draw_lengths(key, part):
    key = jax.random.fold_in(key, 11)
    first_key, second_key = jax.random.split(key)
    drawn = jax.random.randint(first_key, (B,), L_MAX // 4, L_MAX + 1)
    longest = jax.random.randint(second_key, (), 0, B)
    return jnp.where(jnp.arange(B) == longest, L_MAX, drawn).astype(jnp.int32)


def draw_w_q(key, part):
    picked_rows = chosen_heads(key)
    key = jax.random.fold_in(key, 21)
    base = jnp.clip(jax.random.normal(key, (D, H * HD), jnp.float32), -4.0, 4.0)
    column = jnp.arange(H * HD)
    head = column // HD
    group = head // (H // KVH)
    picked = (head == group * (H // KVH) + jnp.take(picked_rows, group)) & (column % HD == HD // 2 - 1)
    factor = jnp.where(picked, 12.0, 1.0).astype(jnp.float32)
    return (base * factor[None, :] * D ** (-0.5)).astype(jnp.bfloat16)


def draw_k_cache(key, part):
    key = jax.random.fold_in(key, 23)
    base_key, place_key, power_key = jax.random.split(key, 3)
    base = jnp.clip(2.5 * jax.random.normal(base_key, (B, L_MAX, KVH, HD), jnp.float32), -10.0, 10.0)
    ceiling = 80.0
    strength = jnp.exp(jax.random.uniform(power_key, (B, KVH), jnp.float32, math.log(16.0), math.log(ceiling)))
    stride = L_MAX // 16
    offsets = jax.random.randint(place_key, (B, 4), 0, stride)
    places = jnp.arange(4)[None, :] * stride + offsets
    signs = jnp.array([1.0, 1.0, -1.0, -1.0], jnp.float32)
    hit = jnp.arange(L_MAX)[None, :, None] == places[:, None, :]
    sign_at = jnp.sum(jnp.where(hit, signs[None, None, :], 0.0), -1)
    planted = (sign_at != 0.0)[:, :, None, None]
    dim_mask = (jnp.arange(HD) == HD // 2 - 1)[None, None, None, :]
    planted_row = jnp.where(dim_mask, sign_at[:, :, None, None] * strength[:, None, :, None], 0.5 * base)
    return jnp.where(planted, planted_row, base).astype(jnp.bfloat16)


def steps_of(stream_key, extent, cuts, smallest, high):
    level = 1.0
    for dim, parts in cuts:
        steps = jax.random.uniform(jax.random.fold_in(jax.random.fold_in(stream_key, 6), dim), (parts,), jnp.float32, smallest / len(cuts), high / len(cuts))
        level = level * jnp.repeat(jnp.exp(steps), extent[dim] // parts).reshape((-1,) + (1,) * (len(extent) - 1 - dim))
    return level


def bell_draw(rng, dims, spread, bound, pieces=(), dtype=jnp.bfloat16):
    entries = spread * jax.random.normal(rng, dims, jnp.float32)
    if pieces:
        entries = entries * steps_of(rng, dims, pieces, -0.22, 0.18)
    return jnp.clip(entries, -bound, bound).astype(dtype)


def setup_inputs(seed: int = 0) -> dict:
    seeds = jax.random.split(jax.random.key(seed), 14)
    return {
        "tokens": bell_draw(seeds[0], (2, B, D), 1.0, 6.0, ((2, 64),)),
        "lengths": draw_lengths(jax.random.fold_in(seeds[13], 71), 0),
        "attn_gain": jnp.clip(1.0 + 0.15 * jax.random.normal(seeds[2], (D,), jnp.float32), 0.25, 1.75).astype(jnp.bfloat16),
        "ffn_gain": jnp.clip(1.0 + 0.15 * jax.random.normal(seeds[3], (D,), jnp.float32), 0.25, 1.75).astype(jnp.bfloat16),
        "w_q": draw_w_q(jax.random.fold_in(seeds[13], 71), 0),
        "w_k": bell_draw(seeds[5], (D, KVH * HD), (D // 16) ** -0.5, 0.25, ((0, 64), (1, 8))),
        "w_v": bell_draw(seeds[6], (D, KVH * HD), (D // 16) ** -0.5, 0.25, ((0, 64), (1, 8))),
        "w_o": bell_draw(seeds[7], (H * HD, D), (H * HD) ** -0.5, 0.0625, ((0, 8), (1, 64))),
        "w_gate": bell_draw(seeds[8], (D, FF), D ** -0.5, 0.0625, ((0, 64), (1, 8))),
        "w_up": bell_draw(seeds[9], (D, FF), D ** -0.5, 0.0625, ((0, 64), (1, 8))),
        "w_down": bell_draw(seeds[10], (FF, D), FF ** -0.5, 0.03125, ((0, 8), (1, 64))),
        "k_cache": draw_k_cache(jax.random.fold_in(seeds[13], 71), 0),
        "v_cache": bell_draw(seeds[12], (B, L_MAX, KVH, HD), 1.0, 6.0, ((1, 64), (2, 8))),
    }


eps_value = 1e-05

def rotary(values, position):
    half = values.shape[-1] // 2
    freq = 500000.0 ** (-(jnp.arange(half).astype(jnp.float32) * 2.0) / values.shape[-1])
    angle = position[..., None].astype(jnp.float32) * freq
    cosine = jnp.cos(angle)
    sine = jnp.sin(angle)
    first = values[..., :half]
    second = values[..., half:]
    return jnp.concatenate([first * cosine - second * sine, second * cosine + first * sine], axis=-1)

def reference(tokens, lengths, attn_gain, ffn_gain, w_q, w_k, w_v, w_o, w_gate, w_up, w_down, k_cache, v_cache):
    ratio = H // KVH
    new_keys = []
    new_values = []
    attended_list = []
    output_list = []
    for step in range(2):
        x = tokens[step].astype(jnp.float32)
        sq_attn = lax.optimization_barrier(jnp.sum(x * x, -1, keepdims=True))
        xg = (x * attn_gain.astype(jnp.float32)).astype(jnp.bfloat16)
        scale_a = lax.rsqrt(sq_attn / D + eps_value)
        q_full = jnp.dot(xg, w_q, preferred_element_type=jnp.float32) * scale_a
        k_full = jnp.dot(xg, w_k, preferred_element_type=jnp.float32) * scale_a
        v_full = jnp.dot(xg, w_v, preferred_element_type=jnp.float32) * scale_a
        position = lengths + step
        queries = rotary(q_full.reshape(B, H, HD), position[:, None]).astype(jnp.bfloat16).reshape(B, KVH, ratio, HD)
        new_keys.append(rotary(k_full.reshape(B, KVH, HD), position[:, None]).astype(jnp.bfloat16))
        new_values.append(v_full.reshape(B, KVH, HD).astype(jnp.bfloat16))
        fresh_k = jnp.stack(new_keys, 2)
        fresh_v = jnp.stack(new_values, 2)

        def one_request(items):
            query, keys, vals, fkeys, fvals, length = items
            qf = query.astype(jnp.float32)
            scores = jnp.einsum('grd,pgd->grp', qf, keys.astype(jnp.float32)) / math.sqrt(HD)
            valid = jnp.arange(L_MAX) < length
            scores = jnp.where(valid[None, None, :], scores, -1e+30)
            fresh = jnp.einsum('grd,gjd->grj', qf, fkeys.astype(jnp.float32)) / math.sqrt(HD)
            top = jnp.maximum(lax.optimization_barrier(jnp.max(scores, -1)), lax.optimization_barrier(jnp.max(fresh, -1)))
            cache_w = jnp.where(valid[None, None, :], jnp.exp(scores - top[..., None]), 0.0)
            fresh_w = jnp.exp(fresh - top[..., None])
            total = lax.optimization_barrier(jnp.sum(cache_w, -1)) + lax.optimization_barrier(jnp.sum(fresh_w, -1))
            acc = jnp.einsum('grp,pgd->grd', cache_w.astype(jnp.bfloat16).astype(jnp.float32), vals.astype(jnp.float32))
            acc = acc + jnp.einsum('grj,gjd->grd', fresh_w.astype(jnp.bfloat16).astype(jnp.float32), fvals.astype(jnp.float32))
            return (acc / total[..., None]).astype(jnp.bfloat16)
        attn = lax.map(one_request, (queries, k_cache, v_cache, fresh_k, fresh_v, lengths))
        attended = jnp.dot(attn.reshape(B, H * HD), w_o, preferred_element_type=jnp.float32)
        x_mid = x + attended
        sq_ffn = lax.optimization_barrier(jnp.sum(x_mid * x_mid, -1, keepdims=True))
        xh = (x_mid * ffn_gain.astype(jnp.float32)).astype(jnp.bfloat16)
        scale_f = lax.rsqrt(sq_ffn / D + eps_value)
        gate = jnp.dot(xh, w_gate, preferred_element_type=jnp.float32) * scale_f
        up_part = jnp.dot(xh, w_up, preferred_element_type=jnp.float32) * scale_f
        hidden = (jax.nn.silu(gate) * up_part).astype(jnp.bfloat16)
        result = x_mid + jnp.dot(hidden, w_down, preferred_element_type=jnp.float32)
        attended_list.append(attended.astype(jnp.bfloat16))
        output_list.append(result.astype(jnp.bfloat16))
    return (jnp.stack(attended_list, 0), jnp.stack(output_list, 0))
```

```python
import math

import jax
import jax.numpy as jnp
import numpy as np
from jax import lax
from jax.experimental import pallas as pl
from jax.experimental.pallas import tpu as pltpu
from jax.sharding import PartitionSpec as P

MESH = pl.DeviceIdType.MESH
D = 8192
EPS = 1e-05
F32 = jnp.float32
BF16 = jnp.bfloat16
FAR_FIRST = (4, 3, 5, 2, 6, 1, 7)
TILES = 28
BLOCK = 512
QKV_RS, QKV_AR, QKV_AG, ATT_RS, ATT_AR, ATT_AG, OUT_AR, SQ_RS, FFN_RS, SQ_AR, FFN_AR, FFN_AG, DOWN_AR = range(13)


def total_of(ref, rows):
    parts = [ref[i, rows, :].astype(F32) for i in range(8)]
    return ((parts[0] + parts[1]) + (parts[2] + parts[3])) + (
        (parts[4] + parts[5]) + (parts[6] + parts[7])
    )


def row_of(column):
    lane = lax.broadcasted_iota(jnp.int32, (8, 128), 1)
    row = lax.broadcasted_iota(jnp.int32, (8, 128), 0)
    return jnp.sum(jnp.where(lane == row, column, 0.0), axis=0, keepdims=True)


def column_of(line):
    lane = lax.broadcasted_iota(jnp.int32, (8, 128), 1)
    row = lax.broadcasted_iota(jnp.int32, (8, 128), 0)
    return jnp.sum(jnp.where(lane == row, line, 0.0), axis=1, keepdims=True)


def merged(ref):
    lane = lax.broadcasted_iota(jnp.int32, (8, 128), 1)
    low = lane < 64
    peaks, totals = [], []
    for i in range(8):
        both = ref[i, 8:16, :]
        turned = pltpu.roll(both, 64, 1)
        peaks.append(jnp.where(low, both, turned))
        totals.append(jnp.where(low, turned, both))
    peak = peaks[0]
    for i in range(1, 8):
        peak = jnp.maximum(peak, peaks[i])
    total = jnp.zeros((8, 128), F32)
    summed = jnp.zeros((8, 128), F32)
    for i in range(8):
        factor = jnp.exp(peaks[i] - peak)
        total += factor * totals[i]
        summed += factor * ref[i, 0:8, :]
    return peak, total, summed


def kernel(
    lengths, tokens, attn_gain, ffn_gain, freq,
    h_q, h_k, h_v, h_o, h_gate, h_up, h_down, h_kc, h_vc,
    attended_ref, layer_ref,
    w_q, w_k, w_v, w_o, w_gate, w_up, w_down, k_c, v_c,
    s_qkv, r_qkv, r_qkv2, r_q,
    heads, sums, peaks,
    s_att, r_att, r_att2, r_attn,
    r_out,
    s_sq, r_sq, r_sq2,
    s_ffn, r_ffn, r_ffn2, r_hid,
    r_down,
    load_sem, send_sem, recv_sem,
):
    ctx = lax.axis_index("ctx")
    kvh = lax.axis_index("kvh")
    xc = lax.rem(ctx, 8)
    z = ctx // 8

    def xc_peer(d):
        to = lax.rem(xc + d, 8)
        return to, (z * 8 + to, kvh)

    def z_peer(d):
        return (lax.rem(z + d, 8) * 8 + xc, kvh)

    def y_peer(d):
        return (ctx, lax.rem(kvh + d, 8))

    def send(src, dst, stage, peer):
        pltpu.make_async_remote_copy(
            src_ref=src, dst_ref=dst, send_sem=send_sem.at[stage], recv_sem=recv_sem.at[stage],
            device_id=peer, device_id_type=MESH,
        ).start()

    def arrived(ref, stage):
        pltpu.make_async_copy(ref, ref, recv_sem.at[stage]).wait()

    loads = {}
    for i, (name, src, dst) in enumerate(
        (
            ("q", h_q, w_q), ("k", h_k, w_k), ("v", h_v, w_v), ("kc", h_kc, k_c), ("vc", h_vc, v_c),
            ("o", h_o, w_o), ("gate", h_gate, w_gate), ("up", h_up, w_up), ("down", h_down, w_down),
        )
    ):
        loads[name] = pltpu.make_async_copy(src, dst, load_sem.at[i])
        loads[name].start()

    barrier = pltpu.get_barrier_semaphore()
    for d in FAR_FIRST:
        for peer in (z_peer(d), y_peer(d), xc_peer(d)[1]):
            pl.semaphore_signal(barrier, inc=1, device_id=peer, device_id_type=MESH)

    x = jnp.concatenate([tokens[0], tokens[1]], axis=0).astype(F32)
    sq = row_of(jnp.sum(x * x, axis=1, keepdims=True))
    xg = (x * attn_gain[...].astype(F32)).astype(BF16)
    for name in ("q", "k", "v"):
        loads[name].wait()
    q_part = jnp.dot(xg, w_q[...], preferred_element_type=F32)
    k_part = jnp.dot(xg, w_k[...], preferred_element_type=F32)
    v_part = jnp.dot(xg, w_v[...], preferred_element_type=F32)
    sq_tile = jnp.broadcast_to(sq, (8, 128))
    for j in range(8):
        s_qkv[j, 0:8, :] = q_part[:, j * 128 : (j + 1) * 128]
        s_qkv[j, 8:16, :] = k_part if j < 4 else v_part
        s_qkv[j, 16:24, :] = sq_tile
    r_qkv[xc] = s_qkv[xc]

    pl.semaphore_wait(barrier, 21)
    for d in FAR_FIRST:
        to, peer = xc_peer(d)
        send(s_qkv.at[to, pl.ds(0, 17)], r_qkv.at[xc, pl.ds(0, 17)], QKV_RS, peer)

    row = lax.broadcasted_iota(jnp.int32, (8, 128), 0)
    lane = lax.broadcasted_iota(jnp.int32, (8, 128), 1)
    position = jnp.where(row >= 4, 1, 0)
    for b in range(4):
        position += jnp.where(lax.rem(row, 4) == b, lengths[b], 0)
    angle = position.astype(F32) * freq[...]
    cosine = jnp.cos(angle)
    sine = jnp.sin(angle)
    sine = jnp.where(lane < 64, -sine, sine)

    def rotary(a):
        return a * cosine + pltpu.roll(a, 64, 1) * sine

    arrived(r_qkv.at[pl.ds(0, 7), pl.ds(0, 17)], QKV_RS)
    r_qkv2[z, 0:16, :] = total_of(r_qkv, pl.ds(0, 16))
    r_qkv2[z, 16:17, :] = total_of(r_qkv, pl.ds(16, 1))
    for d in FAR_FIRST:
        mine = r_qkv2.at[z, pl.ds(0, 17)]
        send(mine, mine, QKV_AR, z_peer(d))
    arrived(r_qkv2.at[pl.ds(0, 7), pl.ds(0, 17)], QKV_AR)
    scale = lax.rsqrt(column_of(total_of(r_qkv2, pl.ds(16, 1))) / D + EPS)
    q_mine = rotary(total_of(r_qkv2, pl.ds(0, 8)) * scale).astype(BF16)
    kv_mine = total_of(r_qkv2, pl.ds(8, 8)) * scale
    kv_mine = jnp.where(xc < 4, rotary(kv_mine), kv_mine).astype(BF16)
    r_q[xc] = jnp.concatenate([q_mine, kv_mine], axis=0)
    for d in FAR_FIRST:
        send(r_q.at[xc], r_q.at[xc], QKV_AG, xc_peer(d)[1])
    q_mine = q_mine.astype(F32)
    loads["kc"].wait()
    loads["vc"].wait()
    arrived(r_q.at[pl.ds(0, 7)], QKV_AG)

    for h in range(8):
        heads[h * 8 : (h + 1) * 8, :] = r_q[h].astype(F32)[0:8, :]
    spot = ctx * 256 + lax.broadcasted_iota(jnp.int32, (16, 256), 1)
    low16 = lax.broadcasted_iota(jnp.int32, (16, 128), 1) < 64
    for b in range(4):
        queries = jnp.concatenate(
            [heads[pl.ds(b, 8, stride=8), :], heads[pl.ds(b + 4, 8, stride=8), :]], axis=0
        ).astype(BF16)
        scores = lax.dot_general(
            queries, k_c[b], (((1,), (1,)), ((), ())), preferred_element_type=F32
        ) / math.sqrt(128)
        valid = spot < lengths[b]
        scores = jnp.where(valid, scores, -1e30)
        peak = jnp.max(scores, axis=1, keepdims=True)
        weights = jnp.where(valid, jnp.exp(scores - peak), 0.0)
        total = jnp.sum(weights, axis=1, keepdims=True)
        acc = jnp.dot(weights.astype(BF16), v_c[b], preferred_element_type=F32)
        both = jnp.where(low16, peak, total)
        for s in range(2):
            at = (s * 4 + b) * 8
            sums[at : at + 8, :] = acc[s * 8 : s * 8 + 8, :]
            peaks[at : at + 8, :] = both[s * 8 : s * 8 + 8, :]
    for h in range(8):
        s_att[h, 0:8, :] = sums[pl.ds(h, 8, stride=8), :]
        s_att[h, 8:16, :] = peaks[pl.ds(h, 8, stride=8), :]
    r_att[xc] = s_att[xc]
    for d in FAR_FIRST:
        to, peer = xc_peer(d)
        send(s_att.at[to], r_att.at[xc], ATT_RS, peer)

    k_new = r_q[0].astype(F32)[8:16, :]
    v_new = r_q[4].astype(F32)[8:16, :]
    k_first = jnp.concatenate([k_new[0:4], k_new[0:4]], axis=0)
    k_second = jnp.concatenate([k_new[4:8], k_new[4:8]], axis=0)
    v_first = jnp.concatenate([v_new[0:4], v_new[0:4]], axis=0)
    v_second = jnp.concatenate([v_new[4:8], v_new[4:8]], axis=0)
    f_first = jnp.sum(q_mine * k_first, axis=1, keepdims=True) / math.sqrt(128)
    f_second = jnp.sum(q_mine * k_second, axis=1, keepdims=True) / math.sqrt(128)
    f_first = jnp.broadcast_to(f_first, (8, 128))
    f_second = jnp.broadcast_to(f_second, (8, 128))
    second = row >= 4
    f_second = jnp.where(second, f_second, -1e30)

    arrived(r_att.at[pl.ds(0, 7)], ATT_RS)
    peak, total, summed = merged(r_att)
    r_att2[z, 0:8, :] = summed
    r_att2[z, 8:16, :] = jnp.where(lane < 64, peak, total)
    for d in FAR_FIRST:
        send(r_att2.at[z], r_att2.at[z], ATT_AR, z_peer(d))
    loads["o"].wait()
    arrived(r_att2.at[pl.ds(0, 7)], ATT_AR)
    peak, total, summed = merged(r_att2)
    top = jnp.maximum(peak, jnp.maximum(f_first, f_second))
    factor = jnp.exp(peak - top)
    e_first = jnp.exp(f_first - top)
    e_second = jnp.where(second, jnp.exp(f_second - top), 0.0)
    total = total * factor + e_first + e_second
    summed = (
        summed * factor
        + e_first.astype(BF16).astype(F32) * v_first
        + e_second.astype(BF16).astype(F32) * v_second
    )
    r_attn[xc] = summed / total
    for d in FAR_FIRST:
        send(r_attn.at[xc], r_attn.at[xc], ATT_AG, xc_peer(d)[1])
    arrived(r_attn.at[pl.ds(0, 7)], ATT_AG)

    attn = jnp.concatenate([r_attn[h] for h in range(8)], axis=1).astype(BF16)
    r_out[kvh] = jnp.dot(attn, w_o[...], preferred_element_type=F32)
    for d in FAR_FIRST:
        send(r_out.at[kvh], r_out.at[kvh], OUT_AR, y_peer(d))
    loads["gate"].wait()
    loads["up"].wait()
    arrived(r_out.at[pl.ds(0, 7)], OUT_AR)
    attended = total_of(r_out, pl.ds(0, 8))
    x_mid = x + attended
    s_sq[...] = jnp.broadcast_to(row_of(jnp.sum(x_mid * x_mid, axis=1, keepdims=True)), (8, 128))
    r_sq[xc] = s_sq[...]
    for d in FAR_FIRST:
        send(s_sq.at[pl.ds(0, 1)], r_sq.at[xc, pl.ds(0, 1)], SQ_RS, xc_peer(d)[1])
    attended_ref[0] = attended[0:4].astype(BF16)
    attended_ref[1] = attended[4:8].astype(BF16)

    xh = (x_mid * ffn_gain[...].astype(F32)).astype(BF16)
    for d in FAR_FIRST + (0,):
        to, peer = xc_peer(d)
        start = pl.multiple_of(((to // 2) * 7 + lax.rem(to, 2) * 3) * 128, 128)
        gate = jnp.dot(xh, w_gate[:, pl.ds(start, BLOCK)], preferred_element_type=F32)
        up = jnp.dot(xh, w_up[:, pl.ds(start, BLOCK)], preferred_element_type=F32)
        both = jnp.concatenate([gate, up], axis=0).astype(BF16)
        if d:
            s_ffn[to] = both
            send(s_ffn.at[to], r_ffn.at[xc], FFN_RS, peer)
        else:
            r_ffn[xc] = both
    arrived(r_sq.at[pl.ds(0, 7), pl.ds(0, 1)], SQ_RS)
    r_sq2[z, 0:1, :] = total_of(r_sq, pl.ds(0, 1))
    for d in FAR_FIRST:
        mine = r_sq2.at[z, pl.ds(0, 1)]
        send(mine, mine, SQ_AR, z_peer(d))
    arrived(r_ffn.at[pl.ds(0, 7)], FFN_RS)
    r_ffn2[z] = total_of(r_ffn, pl.ds(0, 16)).astype(BF16)
    for d in FAR_FIRST:
        send(r_ffn2.at[z], r_ffn2.at[z], FFN_AR, z_peer(d))
    arrived(r_sq2.at[pl.ds(0, 7), pl.ds(0, 1)], SQ_AR)
    scale = lax.rsqrt(column_of(total_of(r_sq2, pl.ds(0, 1))) / D + EPS)
    loads["down"].wait()
    arrived(r_ffn2.at[pl.ds(0, 7)], FFN_AR)
    both = total_of(r_ffn2, pl.ds(0, 16))
    gate = both[0:8] * scale
    hidden = gate / (1.0 + jnp.exp(-gate)) * (both[8:16] * scale)
    r_hid[xc] = jnp.concatenate([hidden[:, 0:256], hidden[:, 256:512]], axis=0).astype(BF16)
    for d in FAR_FIRST:
        send(r_hid.at[xc], r_hid.at[xc], FFN_AG, xc_peer(d)[1])
    arrived(r_hid.at[pl.ds(0, 7)], FFN_AG)

    pieces = []
    for j in range(8):
        piece = r_hid[j].astype(F32)
        if j % 2 == 0:
            pieces.append(piece[0:8])
        else:
            pieces.append(piece[0:8, 128:256])
        pieces.append(piece[8:16])
    r_down[kvh] = jnp.dot(
        jnp.concatenate(pieces, axis=1).astype(BF16), w_down[...], preferred_element_type=F32
    )
    for d in FAR_FIRST:
        send(r_down.at[kvh], r_down.at[kvh], DOWN_AR, y_peer(d))
    sent = (
        (r_qkv.at[pl.ds(0, 7), pl.ds(0, 17)], (QKV_RS, QKV_AR)),
        (r_q.at[pl.ds(0, 7)], (QKV_AG,)),
        (r_att.at[pl.ds(0, 7)], (ATT_RS, ATT_AR)),
        (r_attn.at[pl.ds(0, 7)], (ATT_AG, OUT_AR)),
        (r_sq.at[pl.ds(0, 7), pl.ds(0, 1)], (SQ_RS, SQ_AR)),
        (r_ffn.at[pl.ds(0, 7)], (FFN_RS, FFN_AR)),
        (r_hid.at[pl.ds(0, 7)], (FFN_AG,)),
        (r_down.at[pl.ds(0, 7)], (DOWN_AR,)),
    )
    for ref, stages in sent:
        for stage in stages:
            pltpu.make_async_copy(ref, ref, send_sem.at[stage]).wait()
    arrived(r_down.at[pl.ds(0, 7)], DOWN_AR)
    layer = x_mid + total_of(r_down, pl.ds(0, 8))
    layer_ref[0] = layer[0:4].astype(BF16)
    layer_ref[1] = layer[4:8].astype(BF16)


def body(tokens, lengths, attn_gain, ffn_gain, w_q, w_k, w_v, w_o, w_gate, w_up, w_down, k_cache, v_cache):
    half = np.arange(64, dtype=np.float64)
    freq = np.tile(500000.0 ** (-2.0 * half / 128.0), 2).astype(np.float32)[None]
    k_cache = k_cache.reshape(4, 256, 128)
    v_cache = v_cache.reshape(4, 256, 128)
    vmem = pl.BlockSpec(memory_space=pltpu.VMEM)
    hbm = pl.BlockSpec(memory_space=pl.ANY)
    weights = (w_q, w_k, w_v, w_o, w_gate, w_up, w_down, k_cache, v_cache)
    out = jax.ShapeDtypeStruct((2, 4, 128), BF16)
    return pl.pallas_call(
        kernel,
        out_shape=(out, out),
        in_specs=[pl.BlockSpec(memory_space=pltpu.SMEM)] + [vmem] * 4 + [hbm] * 9,
        out_specs=(vmem, vmem),
        scratch_shapes=[pltpu.VMEM(w.shape, BF16) for w in weights]
        + [
            pltpu.VMEM((8, 24, 128), F32), pltpu.VMEM((8, 24, 128), F32), pltpu.VMEM((8, 24, 128), F32),
            pltpu.VMEM((8, 16, 128), BF16),
            pltpu.VMEM((64, 128), F32), pltpu.VMEM((64, 128), F32), pltpu.VMEM((64, 128), F32),
            pltpu.VMEM((8, 16, 128), F32), pltpu.VMEM((8, 16, 128), F32), pltpu.VMEM((8, 16, 128), F32),
            pltpu.VMEM((8, 8, 128), F32),
            pltpu.VMEM((8, 8, 128), F32),
            pltpu.VMEM((8, 128), F32), pltpu.VMEM((8, 8, 128), F32), pltpu.VMEM((8, 8, 128), F32),
            pltpu.VMEM((8, 16, BLOCK), BF16), pltpu.VMEM((8, 16, BLOCK), BF16), pltpu.VMEM((8, 16, BLOCK), BF16),
            pltpu.VMEM((8, 16, 256), BF16),
            pltpu.VMEM((8, 8, 128), F32),
            pltpu.SemaphoreType.DMA((9,)),
            pltpu.SemaphoreType.DMA((13,)),
            pltpu.SemaphoreType.DMA((13,)),
        ],
        compiler_params=pltpu.CompilerParams(
            collective_id=0, has_side_effects=True, vmem_limit_bytes=63 * 1024 * 1024
        ),
    )(lengths, tokens, attn_gain.reshape(1, 128), ffn_gain.reshape(1, 128), jnp.asarray(freq), *weights)


def solution(mesh):
    return jax.shard_map(
        body,
        mesh=mesh,
        in_specs=(
            P(None, None, "ctx"),
            P(),
            P("ctx"),
            P("ctx"),
            P("ctx", "kvh"),
            P("ctx", "kvh"),
            P("ctx", "kvh"),
            P("kvh", "ctx"),
            P("ctx", "kvh"),
            P("ctx", "kvh"),
            P("kvh", "ctx"),
            P(None, "ctx", "kvh", None),
            P(None, "ctx", "kvh", None),
        ),
        out_specs=(P(None, None, "ctx"), P(None, None, "ctx")),
        check_vma=False,
    )
```

```python
import math

import jax
import jax.numpy as jnp
import numpy as np
from jax import lax
from jax.experimental import pallas as pl
from jax.experimental.pallas import tpu as pltpu
from jax.sharding import PartitionSpec as P

MESH = pl.DeviceIdType.MESH
D = 8192
EPS = 1e-05
F32 = jnp.float32
BF16 = jnp.bfloat16
FAR_FIRST = (4, 3, 5, 2, 6, 1, 7)
TILES = 28
BLOCK = 512
QKV_RS, QKV_AR, K_MOVE, V_MOVE, ATT_RS, ATT_AR, ATT_AG, OUT_AR, SQ_RS, FFN_RS, SQ_AR, FFN_AR, FFN_AG, DOWN_AR = range(14)


def total_of(ref, rows):
    parts = [ref[i, rows, :].astype(F32) for i in range(8)]
    return ((parts[0] + parts[1]) + (parts[2] + parts[3])) + (
        (parts[4] + parts[5]) + (parts[6] + parts[7])
    )


def row_of(column):
    lane = lax.broadcasted_iota(jnp.int32, (8, 128), 1)
    row = lax.broadcasted_iota(jnp.int32, (8, 128), 0)
    return jnp.sum(jnp.where(lane == row, column, 0.0), axis=0, keepdims=True)


def column_of(line):
    lane = lax.broadcasted_iota(jnp.int32, (8, 128), 1)
    row = lax.broadcasted_iota(jnp.int32, (8, 128), 0)
    return jnp.sum(jnp.where(lane == row, line, 0.0), axis=1, keepdims=True)


def merged(partials):
    lane = lax.broadcasted_iota(jnp.int32, (8, 128), 1)
    low = lane < 64
    peaks, totals = [], []
    for part in partials:
        both = part[8:16]
        turned = pltpu.roll(both, 64, 1)
        peaks.append(jnp.where(low, both, turned))
        totals.append(jnp.where(low, turned, both))
    peak = peaks[0]
    for other in peaks[1:]:
        peak = jnp.maximum(peak, other)
    total = jnp.zeros((8, 128), F32)
    summed = jnp.zeros((8, 128), F32)
    for part, one_peak, one_total in zip(partials, peaks, totals):
        factor = jnp.exp(one_peak - peak)
        total += factor * one_total
        summed += factor * part[0:8]
    return peak, total, summed


def kernel(
    h_lengths, h_tokens, h_attn_gain, h_ffn_gain, h_freq,
    h_q, h_k, h_v, h_o, h_gate, h_up, h_down, h_kc, h_vc,
    out_ref,
    lengths, tokens, attn_gain, ffn_gain, freq,
    w_q, w_k, w_v, w_o, w_gate, w_up, w_down, k_c, v_c,
    s_qkv, r_qkv, r_qkv2,
    s_att, r_att, r_att2, r_attn,
    r_out,
    s_sq, r_sq, r_sq2,
    s_ffn, r_ffn, r_ffn2, r_hid,
    r_down,
    load_sem, send_sem, recv_sem,
):
    ctx = lax.axis_index("ctx")
    kvh = lax.axis_index("kvh")
    xc = lax.rem(ctx, 8)
    z = ctx // 8
    x = xc // 2
    c = lax.rem(xc, 2)

    def xc_peer(d):
        to = lax.rem(xc + d, 8)
        return to, (z * 8 + to, kvh)

    def z_peer(d):
        return (lax.rem(z + d, 8) * 8 + xc, kvh)

    def y_peer(d):
        return (ctx, lax.rem(kvh + d, 8))

    other_core = (z * 8 + x * 2 + (1 - c), kvh)

    def send(src, dst, stage, peer):
        pltpu.make_async_remote_copy(
            src_ref=src, dst_ref=dst, send_sem=send_sem.at[stage], recv_sem=recv_sem.at[stage],
            device_id=peer, device_id_type=MESH,
        ).start()

    def arrived(ref, stage):
        pltpu.make_async_copy(ref, ref, recv_sem.at[stage]).wait()

    barrier = pltpu.get_barrier_semaphore()
    for d in FAR_FIRST:
        pl.semaphore_signal(barrier, inc=1, device_id=xc_peer(d)[1], device_id_type=MESH)
    loads = {}
    for i, (name, src, dst) in enumerate(
        (
            ("tokens", h_tokens, tokens), ("attn_gain", h_attn_gain, attn_gain),
            ("q", h_q, w_q), ("k", h_k, w_k), ("v", h_v, w_v),
            ("lengths", h_lengths, lengths), ("freq", h_freq, freq), ("ffn_gain", h_ffn_gain, ffn_gain),
            ("kc", h_kc.at[x], k_c.at[x]), ("vc", h_vc.at[x], v_c.at[x]),
            ("o", h_o, w_o), ("gate", h_gate, w_gate), ("up", h_up, w_up), ("down", h_down, w_down),
        )
    ):
        loads[name] = pltpu.make_async_copy(src, dst, load_sem.at[i])
        loads[name].start()
    for d in FAR_FIRST:
        for peer in (z_peer(d), y_peer(d)):
            pl.semaphore_signal(barrier, inc=1, device_id=peer, device_id_type=MESH)

    loads["tokens"].wait()
    loads["attn_gain"].wait()
    hid = jnp.concatenate([tokens[0], tokens[1]], axis=0).astype(F32)
    sq = jnp.broadcast_to(jnp.sum(hid * hid, axis=1, keepdims=True), (8, 128))
    xg = (hid * attn_gain[...].astype(F32)).astype(BF16)
    for name in ("q", "k", "v"):
        loads[name].wait()
    q_part = jnp.dot(xg, w_q[...], preferred_element_type=F32)
    k_part = jnp.dot(xg, w_k[...], preferred_element_type=F32)
    v_part = jnp.dot(xg, w_v[...], preferred_element_type=F32)
    for s in range(2):
        rows = slice(s * 4, s * 4 + 4)
        for h in range(8):
            s_qkv[pl.ds(s * 8 + h, 4, stride=24), :] = q_part[rows, h * 128 : (h + 1) * 128]
        s_qkv[pl.ds(16 + s, 4, stride=24), :] = k_part[rows]
        s_qkv[pl.ds(18 + s, 4, stride=24), :] = v_part[rows]
        s_qkv[pl.ds(20 + s, 4, stride=24), :] = sq[rows]
    r_qkv[xc, 0:22, :] = s_qkv[pl.ds(pl.multiple_of(x * 24, 8), 22), :]

    pl.semaphore_wait(barrier, 21)
    for d in FAR_FIRST:
        to, peer = xc_peer(d)
        send(
            s_qkv.at[pl.ds(pl.multiple_of((to // 2) * 24, 8), 22)], r_qkv.at[xc, pl.ds(0, 22)], QKV_RS, peer
        )
    for d in (2, 1, 3):
        to = lax.rem(x + d, 4)
        peer = (z * 8 + to * 2 + c, kvh)
        send(h_kc.at[to], k_c.at[x], K_MOVE, peer)
        send(h_vc.at[to], v_c.at[x], V_MOVE, peer)

    loads["lengths"].wait()
    loads["freq"].wait()
    step8 = lax.broadcasted_iota(jnp.int32, (8, 128), 0)
    lane = lax.broadcasted_iota(jnp.int32, (8, 128), 1)
    length = lengths[x]
    angle = (length + step8).astype(F32) * freq[...]
    cosine = jnp.cos(angle)
    sine = jnp.sin(angle)
    sine = jnp.where(lane < 64, -sine, sine)

    arrived(r_qkv.at[pl.ds(0, 7), pl.ds(0, 22)], QKV_RS)
    r_qkv2[z, 0:22, :] = total_of(r_qkv, pl.ds(0, 22))
    for d in FAR_FIRST:
        mine = r_qkv2.at[z, pl.ds(0, 22)]
        send(mine, mine, QKV_AR, z_peer(d))
    arrived(r_qkv2.at[pl.ds(0, 7), pl.ds(0, 22)], QKV_AR)
    whole = total_of(r_qkv2, pl.ds(0, 22))
    queries, new_keys, new_values = [], [], []
    for s in range(2):
        scale = lax.rsqrt(whole[20 + s : 21 + s] / D + EPS)

        def rotary(a):
            return a * cosine[s : s + 1] + pltpu.roll(a, 64, 1) * sine[s : s + 1]

        queries.append(rotary(whole[s * 8 : s * 8 + 8] * scale).astype(BF16))
        key = jnp.broadcast_to(whole[16 + s : 17 + s] * scale, (8, 128))
        new_keys.append(rotary(key).astype(BF16).astype(F32))
        value = jnp.broadcast_to(whole[18 + s : 19 + s] * scale, (8, 128))
        new_values.append(value.astype(BF16).astype(F32))
    both_steps = jnp.concatenate(queries, axis=0)
    loads["kc"].wait()
    loads["vc"].wait()
    arrived(k_c.at[pl.ds(0, 3)], K_MOVE)

    scores, valid = [], []
    for i in range(4):
        scores.append(
            lax.dot_general(both_steps, k_c[i], (((1,), (1,)), ((), ())), preferred_element_type=F32)
            / math.sqrt(128)
        )
        first = (z * 8 + i * 2 + c) * 256
        valid.append(first + lax.broadcasted_iota(jnp.int32, (16, 256), 1) < length)
    scores = jnp.concatenate(scores, axis=1)
    valid = jnp.concatenate(valid, axis=1)
    scores = jnp.where(valid, scores, -1e30)
    peak = jnp.max(scores, axis=1, keepdims=True)
    weights = jnp.where(valid, jnp.exp(scores - peak), 0.0)
    total = jnp.sum(weights, axis=1, keepdims=True)
    weights = weights.astype(BF16)
    arrived(v_c.at[pl.ds(0, 3)], V_MOVE)
    acc = jnp.zeros((16, 128), F32)
    for i in range(4):
        acc += jnp.dot(weights[:, i * 256 : (i + 1) * 256], v_c[i], preferred_element_type=F32)
    both = jnp.where(lax.broadcasted_iota(jnp.int32, (16, 128), 1) < 64, peak, total)
    for s in range(2):
        rows = slice(s * 8, s * 8 + 8)
        s_att[s] = jnp.concatenate([acc[rows], both[rows]], axis=0)
    send(s_att.at[1 - c], r_att.at[0], ATT_RS, other_core)

    q_mine = jnp.where(c == 0, queries[0].astype(F32), queries[1].astype(F32))
    fresh = [jnp.sum(q_mine * key, axis=1, keepdims=True) / math.sqrt(128) for key in new_keys]
    f_first = jnp.broadcast_to(fresh[0], (8, 128))
    f_second = jnp.where(c == 1, jnp.broadcast_to(fresh[1], (8, 128)), -1e30)

    arrived(r_att.at[0], ATT_RS)
    peak, total, summed = merged([s_att[c], r_att[0]])
    r_att2[z, 0:8, :] = summed
    r_att2[z, 8:16, :] = jnp.where(lane < 64, peak, total)
    for d in FAR_FIRST:
        send(r_att2.at[z], r_att2.at[z], ATT_AR, z_peer(d))
    loads["o"].wait()
    arrived(r_att2.at[pl.ds(0, 7)], ATT_AR)
    peak, total, summed = merged([r_att2[i] for i in range(8)])
    top = jnp.maximum(peak, jnp.maximum(f_first, f_second))
    factor = jnp.exp(peak - top)
    e_first = jnp.exp(f_first - top)
    e_second = jnp.where(c == 1, jnp.exp(f_second - top), 0.0)
    total = total * factor + e_first + e_second
    summed = (
        summed * factor
        + e_first.astype(BF16).astype(F32) * new_values[0]
        + e_second.astype(BF16).astype(F32) * new_values[1]
    )
    mine = r_attn.at[pl.ds(pl.multiple_of((c * 4 + x) * 8, 8), 8)]
    mine[...] = summed / total
    for d in FAR_FIRST:
        send(mine, mine, ATT_AG, xc_peer(d)[1])
    arrived(r_attn.at[pl.ds(0, 56)], ATT_AG)

    attn = jnp.concatenate([r_attn[pl.ds(h, 8, stride=8), :] for h in range(8)], axis=1).astype(BF16)
    r_out[kvh] = jnp.dot(attn, w_o[...], preferred_element_type=F32)
    for d in FAR_FIRST:
        send(r_out.at[kvh], r_out.at[kvh], OUT_AR, y_peer(d))
    for name in ("gate", "up", "ffn_gain"):
        loads[name].wait()
    arrived(r_out.at[pl.ds(0, 7)], OUT_AR)
    attended = total_of(r_out, pl.ds(0, 8))
    x_mid = hid + attended
    s_sq[...] = jnp.broadcast_to(row_of(jnp.sum(x_mid * x_mid, axis=1, keepdims=True)), (8, 128))
    r_sq[xc] = s_sq[...]
    for d in FAR_FIRST:
        send(s_sq.at[pl.ds(0, 1)], r_sq.at[xc, pl.ds(0, 1)], SQ_RS, xc_peer(d)[1])

    xh = (x_mid * ffn_gain[...].astype(F32)).astype(BF16)
    for d in FAR_FIRST + (0,):
        to, peer = xc_peer(d)
        start = pl.multiple_of(((to // 2) * 7 + lax.rem(to, 2) * 3) * 128, 128)
        gate = jnp.dot(xh, w_gate[:, pl.ds(start, BLOCK)], preferred_element_type=F32)
        up = jnp.dot(xh, w_up[:, pl.ds(start, BLOCK)], preferred_element_type=F32)
        both = jnp.concatenate([gate, up], axis=0).astype(BF16)
        if d:
            s_ffn[to] = both
            send(s_ffn.at[to], r_ffn.at[xc], FFN_RS, peer)
        else:
            r_ffn[xc] = both
    out_ref[0] = attended[0:4].astype(BF16)
    out_ref[1] = attended[4:8].astype(BF16)
    arrived(r_sq.at[pl.ds(0, 7), pl.ds(0, 1)], SQ_RS)
    r_sq2[z, 0:1, :] = total_of(r_sq, pl.ds(0, 1))
    for d in FAR_FIRST:
        mine = r_sq2.at[z, pl.ds(0, 1)]
        send(mine, mine, SQ_AR, z_peer(d))
    arrived(r_ffn.at[pl.ds(0, 7)], FFN_RS)
    r_ffn2[z] = total_of(r_ffn, pl.ds(0, 16)).astype(BF16)
    for d in FAR_FIRST:
        send(r_ffn2.at[z], r_ffn2.at[z], FFN_AR, z_peer(d))
    arrived(r_sq2.at[pl.ds(0, 7), pl.ds(0, 1)], SQ_AR)
    scale = lax.rsqrt(column_of(total_of(r_sq2, pl.ds(0, 1))) / D + EPS)
    loads["down"].wait()
    arrived(r_ffn2.at[pl.ds(0, 7)], FFN_AR)
    both = total_of(r_ffn2, pl.ds(0, 16))
    gate = both[0:8] * scale
    hidden = gate / (1.0 + jnp.exp(-gate)) * (both[8:16] * scale)
    r_hid[xc] = jnp.concatenate([hidden[:, 0:256], hidden[:, 256:512]], axis=0).astype(BF16)
    for d in FAR_FIRST:
        send(r_hid.at[xc], r_hid.at[xc], FFN_AG, xc_peer(d)[1])
    arrived(r_hid.at[pl.ds(0, 7)], FFN_AG)

    pieces = []
    for j in range(8):
        piece = r_hid[j].astype(F32)
        if j % 2 == 0:
            pieces.append(piece[0:8])
        else:
            pieces.append(piece[0:8, 128:256])
        pieces.append(piece[8:16])
    r_down[kvh] = jnp.dot(
        jnp.concatenate(pieces, axis=1).astype(BF16), w_down[...], preferred_element_type=F32
    )
    for d in FAR_FIRST:
        send(r_down.at[kvh], r_down.at[kvh], DOWN_AR, y_peer(d))
    sent = (
        (r_qkv.at[pl.ds(0, 7), pl.ds(0, 22)], (QKV_RS, QKV_AR)),
        (k_c.at[pl.ds(0, 3)], (K_MOVE, V_MOVE)),
        (r_att.at[0], (ATT_RS,)),
        (r_att2.at[pl.ds(0, 7)], (ATT_AR,)),
        (r_attn.at[pl.ds(0, 56)], (ATT_AG,)),
        (r_out.at[pl.ds(0, 7)], (OUT_AR,)),
        (r_sq.at[pl.ds(0, 7), pl.ds(0, 1)], (SQ_RS, SQ_AR)),
        (r_ffn.at[pl.ds(0, 7)], (FFN_RS, FFN_AR)),
        (r_hid.at[pl.ds(0, 7)], (FFN_AG,)),
        (r_down.at[pl.ds(0, 7)], (DOWN_AR,)),
    )
    for ref, stages in sent:
        for stage in stages:
            pltpu.make_async_copy(ref, ref, send_sem.at[stage]).wait()
    arrived(r_down.at[pl.ds(0, 7)], DOWN_AR)
    layer = x_mid + total_of(r_down, pl.ds(0, 8))
    out_ref[2] = layer[0:4].astype(BF16)
    out_ref[3] = layer[4:8].astype(BF16)


def body(tokens, lengths, attn_gain, ffn_gain, w_q, w_k, w_v, w_o, w_gate, w_up, w_down, k_cache, v_cache):
    half = np.arange(64, dtype=np.float64)
    freq = np.tile(500000.0 ** (-2.0 * half / 128.0), 2).astype(np.float32)[None]
    k_cache = k_cache.reshape(4, 256, 128)
    v_cache = v_cache.reshape(4, 256, 128)
    hbm = pl.BlockSpec(memory_space=pltpu.HBM)
    small = (tokens, attn_gain.reshape(1, 128), ffn_gain.reshape(1, 128), jnp.asarray(freq))
    weights = (w_q, w_k, w_v, w_o, w_gate, w_up, w_down, k_cache, v_cache)
    both = pl.pallas_call(
        kernel,
        out_shape=pltpu.VMEM((4, 4, 128), BF16),
        in_specs=[hbm] * 14,
        out_specs=pl.BlockSpec(memory_space=pltpu.VMEM),
        scratch_shapes=[pltpu.SMEM((4,), jnp.int32)]
        + [pltpu.VMEM(a.shape, a.dtype) for a in small + weights]
        + [
            pltpu.VMEM((96, 128), F32), pltpu.VMEM((8, 24, 128), F32), pltpu.VMEM((8, 24, 128), F32),
            pltpu.VMEM((2, 16, 128), F32), pltpu.VMEM((1, 16, 128), F32), pltpu.VMEM((8, 16, 128), F32),
            pltpu.VMEM((64, 128), F32),
            pltpu.VMEM((8, 8, 128), F32),
            pltpu.VMEM((8, 128), F32), pltpu.VMEM((8, 8, 128), F32), pltpu.VMEM((8, 8, 128), F32),
            pltpu.VMEM((8, 16, BLOCK), BF16), pltpu.VMEM((8, 16, BLOCK), BF16), pltpu.VMEM((8, 16, BLOCK), BF16),
            pltpu.VMEM((8, 16, 256), BF16),
            pltpu.VMEM((8, 8, 128), F32),
            pltpu.SemaphoreType.DMA((14,)),
            pltpu.SemaphoreType.DMA((14,)),
            pltpu.SemaphoreType.DMA((14,)),
        ],
        compiler_params=pltpu.CompilerParams(
            collective_id=0, has_side_effects=True, vmem_limit_bytes=60 * 1024 * 1024
        ),
    )(*[pltpu.with_memory_space_constraint(a, pltpu.HBM) for a in (lengths, *small, *weights)])
    return both[0:2], both[2:4]


def solution(mesh):
    return jax.shard_map(
        body,
        mesh=mesh,
        in_specs=(
            P(None, None, "ctx"),
            P(),
            P("ctx"),
            P("ctx"),
            P("ctx", "kvh"),
            P("ctx", "kvh"),
            P("ctx", "kvh"),
            P("kvh", "ctx"),
            P("ctx", "kvh"),
            P("ctx", "kvh"),
            P("kvh", "ctx"),
            P(None, "ctx", "kvh", None),
            P(None, "ctx", "kvh", None),
        ),
        out_specs=(P(None, None, "ctx"), P(None, None, "ctx")),
        check_vma=False,
    )
```

```python
import math

import jax
import jax.numpy as jnp
import numpy as np
from jax import lax
from jax.experimental import pallas as pl
from jax.experimental.pallas import tpu as pltpu
from jax.sharding import PartitionSpec as P

MESH = pl.DeviceIdType.MESH
D = 8192
EPS = 1e-05
F32 = jnp.float32
BF16 = jnp.bfloat16
FAR_FIRST = (4, 3, 5, 2, 6, 1, 7)
TILES = 28
BLOCK = 512
QKV_RS, QKV_AR, K_MOVE, V_MOVE, ATT_AR, ATT_AG, OUT_AR, SQ_RS, FFN_RS, SQ_AR, FFN_AR, FFN_AG, DOWN_AR = range(13)


def total_of(ref, rows):
    parts = [ref[i, rows, :].astype(F32) for i in range(8)]
    return ((parts[0] + parts[1]) + (parts[2] + parts[3])) + (
        (parts[4] + parts[5]) + (parts[6] + parts[7])
    )


def row_of(column):
    lane = lax.broadcasted_iota(jnp.int32, (8, 128), 1)
    row = lax.broadcasted_iota(jnp.int32, (8, 128), 0)
    return jnp.sum(jnp.where(lane == row, column, 0.0), axis=0, keepdims=True)


def column_of(line):
    lane = lax.broadcasted_iota(jnp.int32, (8, 128), 1)
    row = lax.broadcasted_iota(jnp.int32, (8, 128), 0)
    return jnp.sum(jnp.where(lane == row, line, 0.0), axis=1, keepdims=True)


def merged(ref):
    lines = ref[pl.ds(8, 16, stride=16), :]
    head = lax.broadcasted_iota(jnp.int32, (16, 128), 1) < 8
    peak = jnp.max(lines, axis=0, keepdims=True)
    factors = jnp.where(head, jnp.exp(jnp.where(head, lines - peak, 0.0)), 0.0)
    total = jnp.sum(factors * pltpu.roll(lines, 120, 1), axis=0, keepdims=True)
    terms = [column_of(factors[i : i + 1]) * ref[i * 16 : i * 16 + 8, :] for i in range(16)]
    while len(terms) > 1:
        terms = [a + b for a, b in zip(terms[0::2], terms[1::2])]
    return column_of(peak), column_of(total), terms[0]


def kernel(
    h_lengths, h_tokens, h_attn_gain, h_ffn_gain, h_freq,
    h_q, h_k, h_v, h_o, h_gate, h_up, h_down, h_kc, h_vc,
    out_ref,
    lengths, tokens, attn_gain, ffn_gain, freq,
    w_q, w_k, w_v, w_o, w_gate, w_up, w_down, k_c, v_c,
    s_qkv, r_qkv, r_qkv2,
    s_att, r_att, r_attn,
    r_out,
    s_sq, r_sq, r_sq2,
    s_ffn, r_ffn, r_ffn2, r_hid,
    r_down,
    load_sem, send_sem, recv_sem,
):
    ctx = lax.axis_index("ctx")
    kvh = lax.axis_index("kvh")
    xc = lax.rem(ctx, 8)
    z = ctx // 8
    x = xc // 2
    c = lax.rem(xc, 2)

    def xc_peer(d):
        to = lax.rem(xc + d, 8)
        return to, (z * 8 + to, kvh)

    def z_peer(d):
        return (lax.rem(z + d, 8) * 8 + xc, kvh)

    def y_peer(d):
        return (ctx, lax.rem(kvh + d, 8))

    def zc_peers():
        for d in FAR_FIRST:
            yield c, (lax.rem(z + d, 8) * 8 + xc, kvh)
            yield 1 - c, (lax.rem(z + d, 8) * 8 + x * 2 + (1 - c), kvh)
        yield 1 - c, (z * 8 + x * 2 + (1 - c), kvh)

    def z_other(d):
        return (lax.rem(z + d, 8) * 8 + x * 2 + (1 - c), kvh)

    def send(src, dst, stage, peer):
        pltpu.make_async_remote_copy(
            src_ref=src, dst_ref=dst, send_sem=send_sem.at[stage], recv_sem=recv_sem.at[stage],
            device_id=peer, device_id_type=MESH,
        ).start()

    def arrived(ref, stage):
        pltpu.make_async_copy(ref, ref, recv_sem.at[stage]).wait()

    barrier = pltpu.get_barrier_semaphore()
    for d in FAR_FIRST:
        pl.semaphore_signal(barrier, inc=1, device_id=xc_peer(d)[1], device_id_type=MESH)
    loads = {}
    for i, (name, src, dst) in enumerate(
        (
            ("tokens", h_tokens, tokens), ("attn_gain", h_attn_gain, attn_gain),
            ("q", h_q, w_q), ("k", h_k, w_k), ("v", h_v, w_v),
            ("lengths", h_lengths, lengths), ("freq", h_freq, freq), ("ffn_gain", h_ffn_gain, ffn_gain),
            ("kc", h_kc.at[x], k_c.at[x]), ("vc", h_vc.at[x], v_c.at[x]),
            ("o", h_o, w_o), ("gate", h_gate, w_gate), ("up", h_up, w_up), ("down", h_down, w_down),
        )
    ):
        loads[name] = pltpu.make_async_copy(src, dst, load_sem.at[i])
        loads[name].start()
    for d in FAR_FIRST:
        for peer in (z_peer(d), z_other(d), y_peer(d)):
            pl.semaphore_signal(barrier, inc=1, device_id=peer, device_id_type=MESH)

    loads["tokens"].wait()
    loads["attn_gain"].wait()
    hid = jnp.concatenate([tokens[0], tokens[1]], axis=0).astype(F32)
    sq = jnp.broadcast_to(jnp.sum(hid * hid, axis=1, keepdims=True), (8, 128))
    xg = (hid * attn_gain[...].astype(F32)).astype(BF16)
    for name in ("q", "k", "v"):
        loads[name].wait()
    q_part = jnp.dot(xg, w_q[...], preferred_element_type=F32)
    k_part = jnp.dot(xg, w_k[...], preferred_element_type=F32)
    v_part = jnp.dot(xg, w_v[...], preferred_element_type=F32)
    for h in range(8):
        s_qkv[pl.ds(h, 8, stride=16), :] = q_part[:, h * 128 : (h + 1) * 128]
    s_qkv[pl.ds(8, 8, stride=16), :] = k_part
    s_qkv[pl.ds(9, 8, stride=16), :] = v_part
    s_qkv[pl.ds(10, 8, stride=16), :] = sq

    def row_block(to):
        return pl.ds(pl.multiple_of((lax.rem(to, 2) * 4 + to // 2) * 16, 16), 11)

    r_qkv[xc, 0:11, :] = s_qkv[row_block(xc), :]

    pl.semaphore_wait(barrier, 28)
    for d in FAR_FIRST:
        to, peer = xc_peer(d)
        send(s_qkv.at[row_block(to)], r_qkv.at[xc, pl.ds(0, 11)], QKV_RS, peer)
    for d in (2, 1, 3):
        to = lax.rem(x + d, 4)
        peer = (z * 8 + to * 2 + c, kvh)
        send(h_kc.at[to], k_c.at[x], K_MOVE, peer)

    loads["lengths"].wait()
    loads["freq"].wait()
    step8 = lax.broadcasted_iota(jnp.int32, (8, 128), 0)
    lane = lax.broadcasted_iota(jnp.int32, (8, 128), 1)
    length = lengths[x]
    angle = (length + step8).astype(F32) * freq[...]
    cosine = jnp.cos(angle)
    sine = jnp.sin(angle)
    sine = jnp.where(lane < 64, -sine, sine)

    arrived(r_qkv.at[pl.ds(0, 7), pl.ds(0, 11)], QKV_RS)
    r_qkv2[z * 2 + c, 0:11, :] = total_of(r_qkv, pl.ds(0, 11))
    mine = r_qkv2.at[z * 2 + c, pl.ds(0, 11)]
    for _, peer in zc_peers():
        send(mine, mine, QKV_AR, peer)
    for d in (2, 1, 3):
        to = lax.rem(x + d, 4)
        send(h_vc.at[to], v_c.at[x], V_MOVE, (z * 8 + to * 2 + c, kvh))
    arrived(r_qkv2.at[pl.ds(0, 15), pl.ds(0, 11)], QKV_AR)
    queries, new_keys, new_values = [], [], []
    for s in range(2):
        parts = [r_qkv2[i * 2 + s, 0:11, :] for i in range(8)]
        while len(parts) > 1:
            parts = [a + b for a, b in zip(parts[0::2], parts[1::2])]
        whole = parts[0]
        scale = lax.rsqrt(whole[10:11] / D + EPS)

        def rotary(a):
            return a * cosine[s : s + 1] + pltpu.roll(a, 64, 1) * sine[s : s + 1]

        queries.append(rotary(whole[0:8] * scale).astype(BF16))
        key = jnp.broadcast_to(whole[8:9] * scale, (8, 128))
        new_keys.append(rotary(key).astype(BF16).astype(F32))
        value = jnp.broadcast_to(whole[9:10] * scale, (8, 128))
        new_values.append(value.astype(BF16).astype(F32))
    both_steps = jnp.concatenate(queries, axis=0)
    loads["kc"].wait()
    loads["vc"].wait()
    arrived(k_c.at[pl.ds(0, 3)], K_MOVE)

    scores, valid = [], []
    for i in range(4):
        scores.append(
            lax.dot_general(both_steps, k_c[i], (((1,), (1,)), ((), ())), preferred_element_type=F32)
            / math.sqrt(128)
        )
        first = (z * 8 + i * 2 + c) * 256
        valid.append(first + lax.broadcasted_iota(jnp.int32, (16, 256), 1) < length)
    scores = jnp.concatenate(scores, axis=1)
    valid = jnp.concatenate(valid, axis=1)
    scores = jnp.where(valid, scores, -1e30)
    peak = jnp.max(scores, axis=1, keepdims=True)
    weights = jnp.where(valid, jnp.exp(scores - peak), 0.0)
    total = jnp.sum(weights, axis=1, keepdims=True)
    weights = weights.astype(BF16)
    arrived(v_c.at[pl.ds(0, 3)], V_MOVE)
    acc = jnp.zeros((16, 128), F32)
    for i in range(4):
        acc += jnp.dot(weights[:, i * 256 : (i + 1) * 256], v_c[i], preferred_element_type=F32)
    for s in range(2):
        rows = slice(s * 8, s * 8 + 8)
        s_att[s, 0:8, :] = acc[rows]
        line = jnp.where(lane == step8, peak[rows], jnp.where(lane == step8 + 8, total[rows], 0.0))
        s_att[s, 8:9, :] = jnp.sum(line, axis=0, keepdims=True)
    slot = pl.ds(pl.multiple_of((z * 2 + c) * 16, 16), 9)
    r_att[slot, :] = s_att[c, 0:9, :]
    for core, peer in zc_peers():
        send(s_att.at[core, pl.ds(0, 9)], r_att.at[slot], ATT_AR, peer)

    q_mine = jnp.where(c == 0, queries[0].astype(F32), queries[1].astype(F32))
    fresh = [jnp.sum(q_mine * key, axis=1, keepdims=True) / math.sqrt(128) for key in new_keys]
    f_first = jnp.broadcast_to(fresh[0], (8, 128))
    f_second = jnp.where(c == 1, jnp.broadcast_to(fresh[1], (8, 128)), -1e30)

    loads["o"].wait()
    arrived(r_att.at[pl.ds(0, 15 * 9)], ATT_AR)
    peak, total, summed = merged(r_att)
    top = jnp.maximum(peak, jnp.maximum(f_first, f_second))
    factor = jnp.exp(peak - top)
    e_first = jnp.exp(f_first - top)
    e_second = jnp.where(c == 1, jnp.exp(f_second - top), 0.0)
    total = total * factor + e_first + e_second
    summed = (
        summed * factor
        + e_first.astype(BF16).astype(F32) * new_values[0]
        + e_second.astype(BF16).astype(F32) * new_values[1]
    )
    mine = r_attn.at[pl.ds(pl.multiple_of((c * 4 + x) * 8, 8), 8)]
    mine[...] = summed / total
    for d in FAR_FIRST:
        send(mine, mine, ATT_AG, xc_peer(d)[1])
    arrived(r_attn.at[pl.ds(0, 56)], ATT_AG)

    attn = jnp.concatenate([r_attn[pl.ds(h, 8, stride=8), :] for h in range(8)], axis=1).astype(BF16)
    r_out[kvh] = jnp.dot(attn, w_o[...], preferred_element_type=F32)
    for d in FAR_FIRST:
        send(r_out.at[kvh], r_out.at[kvh], OUT_AR, y_peer(d))
    for name in ("gate", "up", "ffn_gain"):
        loads[name].wait()
    arrived(r_out.at[pl.ds(0, 7)], OUT_AR)
    attended = total_of(r_out, pl.ds(0, 8))
    x_mid = hid + attended
    s_sq[...] = jnp.broadcast_to(row_of(jnp.sum(x_mid * x_mid, axis=1, keepdims=True)), (8, 128))
    r_sq[xc] = s_sq[...]
    for d in FAR_FIRST:
        send(s_sq.at[pl.ds(0, 1)], r_sq.at[xc, pl.ds(0, 1)], SQ_RS, xc_peer(d)[1])

    xh = (x_mid * ffn_gain[...].astype(F32)).astype(BF16)
    for d in FAR_FIRST + (0,):
        to, peer = xc_peer(d)
        start = pl.multiple_of(((to // 2) * 7 + lax.rem(to, 2) * 3) * 128, 128)
        gate = jnp.dot(xh, w_gate[:, pl.ds(start, BLOCK)], preferred_element_type=F32)
        up = jnp.dot(xh, w_up[:, pl.ds(start, BLOCK)], preferred_element_type=F32)
        both = jnp.concatenate([gate, up], axis=0).astype(BF16)
        if d:
            s_ffn[to] = both
            send(s_ffn.at[to], r_ffn.at[xc], FFN_RS, peer)
        else:
            r_ffn[xc] = both
    out_ref[0] = attended[0:4].astype(BF16)
    out_ref[1] = attended[4:8].astype(BF16)
    arrived(r_sq.at[pl.ds(0, 7), pl.ds(0, 1)], SQ_RS)
    r_sq2[z, 0:1, :] = total_of(r_sq, pl.ds(0, 1))
    for d in FAR_FIRST:
        mine = r_sq2.at[z, pl.ds(0, 1)]
        send(mine, mine, SQ_AR, z_peer(d))
    arrived(r_ffn.at[pl.ds(0, 7)], FFN_RS)
    r_ffn2[z] = total_of(r_ffn, pl.ds(0, 16)).astype(BF16)
    for d in FAR_FIRST:
        send(r_ffn2.at[z], r_ffn2.at[z], FFN_AR, z_peer(d))
    arrived(r_sq2.at[pl.ds(0, 7), pl.ds(0, 1)], SQ_AR)
    scale = lax.rsqrt(column_of(total_of(r_sq2, pl.ds(0, 1))) / D + EPS)
    loads["down"].wait()
    arrived(r_ffn2.at[pl.ds(0, 7)], FFN_AR)
    both = total_of(r_ffn2, pl.ds(0, 16))
    gate = both[0:8] * scale
    hidden = gate / (1.0 + jnp.exp(-gate)) * (both[8:16] * scale)
    r_hid[xc] = jnp.concatenate([hidden[:, 0:256], hidden[:, 256:512]], axis=0).astype(BF16)
    for d in FAR_FIRST:
        send(r_hid.at[xc], r_hid.at[xc], FFN_AG, xc_peer(d)[1])
    arrived(r_hid.at[pl.ds(0, 7)], FFN_AG)

    pieces = []
    for j in range(8):
        piece = r_hid[j].astype(F32)
        if j % 2 == 0:
            pieces.append(piece[0:8])
        else:
            pieces.append(piece[0:8, 128:256])
        pieces.append(piece[8:16])
    r_down[kvh] = jnp.dot(
        jnp.concatenate(pieces, axis=1).astype(BF16), w_down[...], preferred_element_type=F32
    )
    for d in FAR_FIRST:
        send(r_down.at[kvh], r_down.at[kvh], DOWN_AR, y_peer(d))
    sent = (
        (r_qkv.at[pl.ds(0, 7), pl.ds(0, 11)], (QKV_RS,)),
        (r_qkv2.at[pl.ds(0, 15), pl.ds(0, 11)], (QKV_AR,)),
        (k_c.at[pl.ds(0, 3)], (K_MOVE, V_MOVE)),
        (r_att.at[pl.ds(0, 15 * 9)], (ATT_AR,)),
        (r_attn.at[pl.ds(0, 56)], (ATT_AG,)),
        (r_out.at[pl.ds(0, 7)], (OUT_AR,)),
        (r_sq.at[pl.ds(0, 7), pl.ds(0, 1)], (SQ_RS, SQ_AR)),
        (r_ffn.at[pl.ds(0, 7)], (FFN_RS, FFN_AR)),
        (r_hid.at[pl.ds(0, 7)], (FFN_AG,)),
        (r_down.at[pl.ds(0, 7)], (DOWN_AR,)),
    )
    for ref, stages in sent:
        for stage in stages:
            pltpu.make_async_copy(ref, ref, send_sem.at[stage]).wait()
    arrived(r_down.at[pl.ds(0, 7)], DOWN_AR)
    layer = x_mid + total_of(r_down, pl.ds(0, 8))
    out_ref[2] = layer[0:4].astype(BF16)
    out_ref[3] = layer[4:8].astype(BF16)


def body(tokens, lengths, attn_gain, ffn_gain, w_q, w_k, w_v, w_o, w_gate, w_up, w_down, k_cache, v_cache):
    half = np.arange(64, dtype=np.float64)
    freq = np.tile(500000.0 ** (-2.0 * half / 128.0), 2).astype(np.float32)[None]
    k_cache = k_cache.reshape(4, 256, 128)
    v_cache = v_cache.reshape(4, 256, 128)
    hbm = pl.BlockSpec(memory_space=pltpu.HBM)
    small = (tokens, attn_gain.reshape(1, 128), ffn_gain.reshape(1, 128), jnp.asarray(freq))
    weights = (w_q, w_k, w_v, w_o, w_gate, w_up, w_down, k_cache, v_cache)
    both = pl.pallas_call(
        kernel,
        out_shape=pltpu.VMEM((4, 4, 128), BF16),
        in_specs=[hbm] * 14,
        out_specs=pl.BlockSpec(memory_space=pltpu.VMEM),
        scratch_shapes=[pltpu.SMEM((4,), jnp.int32)]
        + [pltpu.VMEM(a.shape, a.dtype) for a in small + weights]
        + [
            pltpu.VMEM((128, 128), F32), pltpu.VMEM((8, 16, 128), F32), pltpu.VMEM((16, 16, 128), F32),
            pltpu.VMEM((2, 16, 128), F32), pltpu.VMEM((256, 128), F32),
            pltpu.VMEM((64, 128), F32),
            pltpu.VMEM((8, 8, 128), F32),
            pltpu.VMEM((8, 128), F32), pltpu.VMEM((8, 8, 128), F32), pltpu.VMEM((8, 8, 128), F32),
            pltpu.VMEM((8, 16, BLOCK), BF16), pltpu.VMEM((8, 16, BLOCK), BF16), pltpu.VMEM((8, 16, BLOCK), BF16),
            pltpu.VMEM((8, 16, 256), BF16),
            pltpu.VMEM((8, 8, 128), F32),
            pltpu.SemaphoreType.DMA((14,)),
            pltpu.SemaphoreType.DMA((13,)),
            pltpu.SemaphoreType.DMA((13,)),
        ],
        compiler_params=pltpu.CompilerParams(
            collective_id=0, has_side_effects=True, vmem_limit_bytes=60 * 1024 * 1024
        ),
    )(*[pltpu.with_memory_space_constraint(a, pltpu.HBM) for a in (lengths, *small, *weights)])
    return both[0:2], both[2:4]


def solution(mesh):
    return jax.shard_map(
        body,
        mesh=mesh,
        in_specs=(
            P(None, None, "ctx"),
            P(),
            P("ctx"),
            P("ctx"),
            P("ctx", "kvh"),
            P("ctx", "kvh"),
            P("ctx", "kvh"),
            P("kvh", "ctx"),
            P("ctx", "kvh"),
            P("ctx", "kvh"),
            P("kvh", "ctx"),
            P(None, "ctx", "kvh", None),
            P(None, "ctx", "kvh", None),
        ),
        out_specs=(P(None, None, "ctx"), P(None, None, "ctx")),
        check_vma=False,
    )
```

```python
import math

import jax
import jax.numpy as jnp
import numpy as np
from jax import lax
from jax.experimental import pallas as pl
from jax.experimental.pallas import tpu as pltpu
from jax.sharding import PartitionSpec as P

MESH = pl.DeviceIdType.MESH
D = 8192
EPS = 1e-05
F32 = jnp.float32
BF16 = jnp.bfloat16
FAR_FIRST = (4, 3, 5, 2, 6, 1, 7)
RING = ((2, 0), (2, 1), (1, 0), (3, 0), (1, 1), (3, 1), (0, 1))
TILES = 28
BLOCK = 512
QKV_RS, QKV_AR, K_MOVE, V_MOVE, ATT_AR, ATT_AG, OUT_AR, FFN_RS, FFN_AR, FFN_AG, DOWN_AR = range(11)


def total_of(ref, rows):
    parts = [ref[i, rows, :].astype(F32) for i in range(8)]
    return ((parts[0] + parts[1]) + (parts[2] + parts[3])) + (
        (parts[4] + parts[5]) + (parts[6] + parts[7])
    )


def column_of(line):
    lane = lax.broadcasted_iota(jnp.int32, (8, 128), 1)
    row = lax.broadcasted_iota(jnp.int32, (8, 128), 0)
    return jnp.sum(jnp.where(lane == row, line, 0.0), axis=1, keepdims=True)


def with_square(both, square, core):
    lane = lax.broadcasted_iota(jnp.int32, (16, 128), 1)
    high = square.astype(BF16).astype(F32)
    terms = jnp.concatenate([high, square - high], axis=0)
    first = jnp.where((core == 1) & (lane < 64), terms, both[:, 0:128])
    last = jnp.where((core == 0) & (lane >= 64), terms, both[:, 384:512])
    return jnp.concatenate([first, both[:, 128:384], last], axis=1)


def square_of(both, core):
    lane = lax.broadcasted_iota(jnp.int32, (16, 128), 1)
    tile = jnp.where(core == 1, both[:, 0:128], pltpu.roll(both[:, 384:512], 64, 1))
    tile = jnp.where(lane < 64, tile, pltpu.roll(tile, 64, 1))
    return tile[0:8] + tile[8:16]


def merged(ref):
    lines = ref[pl.ds(8, 16, stride=16), :]
    head = lax.broadcasted_iota(jnp.int32, (16, 128), 1) < 8
    peak = jnp.max(lines, axis=0, keepdims=True)
    factors = jnp.where(head, jnp.exp(jnp.where(head, lines - peak, 0.0)), 0.0)
    total = jnp.sum(factors * pltpu.roll(lines, 120, 1), axis=0, keepdims=True)
    terms = [column_of(factors[i : i + 1]) * ref[i * 16 : i * 16 + 8, :] for i in range(16)]
    while len(terms) > 1:
        terms = [a + b for a, b in zip(terms[0::2], terms[1::2])]
    return column_of(peak), column_of(total), terms[0]


def kernel(
    h_lengths, h_tokens, h_attn_gain, h_ffn_gain, h_freq,
    h_q, h_k, h_v, h_o, h_gate, h_up, h_down, h_kc, h_vc,
    out_ref,
    lengths, tokens, attn_gain, ffn_gain, freq,
    w_q, w_k, w_v, w_o, w_gate, w_up, w_down, k_c, v_c,
    s_qkv, r_qkv, r_qkv2,
    s_att, r_att, r_attn,
    r_out,
    s_ffn, r_ffn, r_ffn2, r_hid,
    r_down,
    load_sem, send_sem, recv_sem, near_sem,
):
    ctx = lax.axis_index("ctx")
    kvh = lax.axis_index("kvh")
    xc = lax.rem(ctx, 8)
    z = ctx // 8
    x = xc // 2
    c = lax.rem(xc, 2)

    def xc_peer(step):
        dx, dc = step
        to = lax.rem(x + dx, 4) * 2 + lax.rem(c + dc, 2)
        return to, (z * 8 + to, kvh)

    def z_peer(d):
        return (lax.rem(z + d, 8) * 8 + xc, kvh)

    def z_other(d):
        return (lax.rem(z + d, 8) * 8 + x * 2 + (1 - c), kvh)

    def y_peer(d):
        return (ctx, lax.rem(kvh + d, 8))

    def zc_peers():
        for d in FAR_FIRST:
            yield c, (lax.rem(z + d, 8) * 8 + xc, kvh)
            yield 1 - c, (lax.rem(z + d, 8) * 8 + x * 2 + (1 - c), kvh)
        yield 1 - c, (z * 8 + x * 2 + (1 - c), kvh)

    def send(src, dst, stage, peer):
        pltpu.make_async_remote_copy(
            src_ref=src, dst_ref=dst, send_sem=send_sem.at[stage], recv_sem=recv_sem.at[stage],
            device_id=peer, device_id_type=MESH,
        ).start()

    def arrived(ref, stage):
        pltpu.make_async_copy(ref, ref, recv_sem.at[stage]).wait()

    barrier = pltpu.get_barrier_semaphore()
    near = [peer(d) for peer in (z_peer, z_other, y_peer) for d in (1, 7)]
    for peer in near + [xc_peer(d)[1] for d in RING]:
        pl.semaphore_signal(barrier, inc=1, device_id=peer, device_id_type=MESH)

    def tell(i, peer_at):
        for d in (1, 7):
            pl.semaphore_signal(near_sem.at[i], inc=1, device_id=peer_at(d), device_id_type=MESH)

    def heard(i):
        pl.semaphore_wait(near_sem.at[i], 2)

    loads = {}
    for i, (name, src, dst) in enumerate(
        (
            ("tokens", h_tokens, tokens), ("attn_gain", h_attn_gain, attn_gain),
            ("q", h_q, w_q), ("k", h_k, w_k), ("v", h_v, w_v),
            ("lengths", h_lengths, lengths), ("freq", h_freq, freq), ("ffn_gain", h_ffn_gain, ffn_gain),
            ("kc", h_kc.at[x], k_c.at[x]), ("vc", h_vc.at[x], v_c.at[x]),
            ("o", h_o, w_o), ("gate", h_gate, w_gate), ("up", h_up, w_up), ("down", h_down, w_down),
        )
    ):
        loads[name] = pltpu.make_async_copy(src, dst, load_sem.at[i])
        loads[name].start()
    loads["tokens"].wait()
    loads["attn_gain"].wait()
    hid = jnp.concatenate([tokens[0], tokens[1]], axis=0).astype(F32)
    sq = jnp.broadcast_to(jnp.sum(hid * hid, axis=1, keepdims=True), (8, 128))
    xg = (hid * attn_gain[...].astype(F32)).astype(BF16)
    for name in ("q", "k", "v"):
        loads[name].wait()
    q_part = jnp.dot(xg, w_q[...], preferred_element_type=F32)
    k_part = jnp.dot(xg, w_k[...], preferred_element_type=F32)
    v_part = jnp.dot(xg, w_v[...], preferred_element_type=F32)
    for h in range(8):
        s_qkv[pl.ds(h, 8, stride=16), :] = q_part[:, h * 128 : (h + 1) * 128]
    s_qkv[pl.ds(8, 8, stride=16), :] = k_part
    s_qkv[pl.ds(9, 8, stride=16), :] = v_part
    s_qkv[pl.ds(10, 8, stride=16), :] = sq

    def row_block(to):
        return pl.ds(pl.multiple_of((lax.rem(to, 2) * 4 + to // 2) * 16, 16), 11)

    r_qkv[xc, 0:11, :] = s_qkv[row_block(xc), :]

    pl.semaphore_wait(barrier, 13)
    tell(0, z_peer)
    for d in RING:
        to, peer = xc_peer(d)
        send(s_qkv.at[row_block(to)], r_qkv.at[xc, pl.ds(0, 11)], QKV_RS, peer)
    for d in (2, 1, 3):
        to = lax.rem(x + d, 4)
        peer = (z * 8 + to * 2 + c, kvh)
        send(h_kc.at[to], k_c.at[x], K_MOVE, peer)

    heard(0)
    tell(1, z_peer)

    loads["lengths"].wait()
    loads["freq"].wait()
    step8 = lax.broadcasted_iota(jnp.int32, (8, 128), 0)
    lane = lax.broadcasted_iota(jnp.int32, (8, 128), 1)
    length = lengths[x]
    angle = (length + step8).astype(F32) * freq[...]
    cosine = jnp.cos(angle)
    sine = jnp.sin(angle)
    sine = jnp.where(lane < 64, -sine, sine)

    heard(1)
    tell(2, z_peer)
    heard(2)
    tell(3, y_peer)
    arrived(r_qkv.at[pl.ds(0, 7), pl.ds(0, 11)], QKV_RS)
    r_qkv2[z * 2 + c, 0:11, :] = total_of(r_qkv, pl.ds(0, 11))
    mine = r_qkv2.at[z * 2 + c, pl.ds(0, 11)]
    for _, peer in zc_peers():
        send(mine, mine, QKV_AR, peer)
    for d in (2, 1, 3):
        to = lax.rem(x + d, 4)
        send(h_vc.at[to], v_c.at[x], V_MOVE, (z * 8 + to * 2 + c, kvh))
    heard(3)
    tell(4, y_peer)
    arrived(r_qkv2.at[pl.ds(0, 15), pl.ds(0, 11)], QKV_AR)
    queries, new_keys, new_values = [], [], []
    for s in range(2):
        parts = [r_qkv2[i * 2 + s, 0:11, :] for i in range(8)]
        while len(parts) > 1:
            parts = [a + b for a, b in zip(parts[0::2], parts[1::2])]
        whole = parts[0]
        scale = lax.rsqrt(whole[10:11] / D + EPS)

        def rotary(a):
            return a * cosine[s : s + 1] + pltpu.roll(a, 64, 1) * sine[s : s + 1]

        queries.append(rotary(whole[0:8] * scale).astype(BF16))
        key = jnp.broadcast_to(whole[8:9] * scale, (8, 128))
        new_keys.append(rotary(key).astype(BF16).astype(F32))
        value = jnp.broadcast_to(whole[9:10] * scale, (8, 128))
        new_values.append(value.astype(BF16).astype(F32))
    both_steps = jnp.concatenate(queries, axis=0)
    loads["kc"].wait()
    loads["vc"].wait()
    arrived(k_c.at[pl.ds(0, 3)], K_MOVE)

    scores, valid = [], []
    for i in range(4):
        scores.append(
            lax.dot_general(both_steps, k_c[i], (((1,), (1,)), ((), ())), preferred_element_type=F32)
            / math.sqrt(128)
        )
        first = (z * 8 + i * 2 + c) * 256
        valid.append(first + lax.broadcasted_iota(jnp.int32, (16, 256), 1) < length)
    scores = jnp.concatenate(scores, axis=1)
    valid = jnp.concatenate(valid, axis=1)
    scores = jnp.where(valid, scores, -1e30)
    peak = jnp.max(scores, axis=1, keepdims=True)
    weights = jnp.where(valid, jnp.exp(scores - peak), 0.0)
    total = jnp.sum(weights, axis=1, keepdims=True)
    weights = weights.astype(BF16)
    arrived(v_c.at[pl.ds(0, 3)], V_MOVE)
    acc = jnp.zeros((16, 128), F32)
    for i in range(4):
        acc += jnp.dot(weights[:, i * 256 : (i + 1) * 256], v_c[i], preferred_element_type=F32)
    for s in range(2):
        rows = slice(s * 8, s * 8 + 8)
        s_att[s, 0:8, :] = acc[rows]
        line = jnp.where(lane == step8, peak[rows], jnp.where(lane == step8 + 8, total[rows], 0.0))
        s_att[s, 8:9, :] = jnp.sum(line, axis=0, keepdims=True)
    slot = pl.ds(pl.multiple_of((z * 2 + c) * 16, 16), 9)
    r_att[slot, :] = s_att[c, 0:9, :]
    for core, peer in zc_peers():
        send(s_att.at[core, pl.ds(0, 9)], r_att.at[slot], ATT_AR, peer)

    q_mine = jnp.where(c == 0, queries[0].astype(F32), queries[1].astype(F32))
    fresh = [jnp.sum(q_mine * key, axis=1, keepdims=True) / math.sqrt(128) for key in new_keys]
    f_first = jnp.broadcast_to(fresh[0], (8, 128))
    f_second = jnp.where(c == 1, jnp.broadcast_to(fresh[1], (8, 128)), -1e30)

    heard(4)
    tell(5, y_peer)
    heard(5)
    loads["o"].wait()
    arrived(r_att.at[pl.ds(0, 15 * 9)], ATT_AR)
    peak, total, summed = merged(r_att)
    top = jnp.maximum(peak, jnp.maximum(f_first, f_second))
    factor = jnp.exp(peak - top)
    e_first = jnp.exp(f_first - top)
    e_second = jnp.where(c == 1, jnp.exp(f_second - top), 0.0)
    total = total * factor + e_first + e_second
    summed = (
        summed * factor
        + e_first.astype(BF16).astype(F32) * new_values[0]
        + e_second.astype(BF16).astype(F32) * new_values[1]
    )
    mine = r_attn.at[pl.ds(pl.multiple_of((c * 4 + x) * 8, 8), 8)]
    mine[...] = summed / total
    for d in RING:
        send(mine, mine, ATT_AG, xc_peer(d)[1])
    arrived(r_attn.at[pl.ds(0, 56)], ATT_AG)

    attn = jnp.concatenate([r_attn[pl.ds(h, 8, stride=8), :] for h in range(8)], axis=1).astype(BF16)
    r_out[kvh] = jnp.dot(attn, w_o[...], preferred_element_type=F32)
    for d in FAR_FIRST:
        send(r_out.at[kvh], r_out.at[kvh], OUT_AR, y_peer(d))
    for name in ("gate", "up", "ffn_gain"):
        loads[name].wait()
    arrived(r_out.at[pl.ds(0, 7)], OUT_AR)
    attended = total_of(r_out, pl.ds(0, 8))
    x_mid = hid + attended
    square = jnp.broadcast_to(jnp.sum(x_mid * x_mid, axis=1, keepdims=True), (8, 128))

    xh = (x_mid * ffn_gain[...].astype(F32)).astype(BF16)
    for d in RING + ((0, 0),):
        to, peer = xc_peer(d)
        start = pl.multiple_of(((to // 2) * 7 + lax.rem(to, 2) * 3) * 128, 128)
        gate = jnp.dot(xh, w_gate[:, pl.ds(start, BLOCK)], preferred_element_type=F32)
        up = jnp.dot(xh, w_up[:, pl.ds(start, BLOCK)], preferred_element_type=F32)
        both = with_square(jnp.concatenate([gate, up], axis=0), square, lax.rem(to, 2)).astype(BF16)
        if d != (0, 0):
            s_ffn[to] = both
            send(s_ffn.at[to], r_ffn.at[xc], FFN_RS, peer)
        else:
            r_ffn[xc] = both
    out_ref[0] = attended[0:4].astype(BF16)
    out_ref[1] = attended[4:8].astype(BF16)
    arrived(r_ffn.at[pl.ds(0, 7)], FFN_RS)
    both = total_of(r_ffn, pl.ds(0, 16))
    r_ffn2[z] = with_square(both, square_of(both, c), c).astype(BF16)
    for d in FAR_FIRST:
        send(r_ffn2.at[z], r_ffn2.at[z], FFN_AR, z_peer(d))
    loads["down"].wait()
    arrived(r_ffn2.at[pl.ds(0, 7)], FFN_AR)
    both = total_of(r_ffn2, pl.ds(0, 16))
    scale = lax.rsqrt(square_of(both, c) / D + EPS)[:, 0:1]
    gate = both[0:8] * scale
    hidden = gate / (1.0 + jnp.exp(-gate)) * (both[8:16] * scale)
    unit = lax.broadcasted_iota(jnp.int32, (8, BLOCK), 1)
    hidden = jnp.where((unit >= c * 64) & (unit < 448 + c * 64), hidden, 0.0)
    r_hid[xc] = jnp.concatenate([hidden[:, 0:256], hidden[:, 256:512]], axis=0).astype(BF16)
    for d in RING:
        send(r_hid.at[xc], r_hid.at[xc], FFN_AG, xc_peer(d)[1])
    arrived(r_hid.at[pl.ds(0, 7)], FFN_AG)

    pieces = []
    for j in range(4):
        even = r_hid[2 * j].astype(F32)
        odd = r_hid[2 * j + 1].astype(F32)
        pieces += [
            even[0:8], even[8:16, 0:128], even[8:16, 128:256] + odd[0:8, 0:128], odd[0:8, 128:256], odd[8:16]
        ]
    r_down[kvh] = jnp.dot(
        jnp.concatenate(pieces, axis=1).astype(BF16), w_down[...], preferred_element_type=F32
    )
    for d in FAR_FIRST:
        send(r_down.at[kvh], r_down.at[kvh], DOWN_AR, y_peer(d))
    sent = (
        (r_qkv.at[pl.ds(0, 7), pl.ds(0, 11)], (QKV_RS,)),
        (r_qkv2.at[pl.ds(0, 15), pl.ds(0, 11)], (QKV_AR,)),
        (k_c.at[pl.ds(0, 3)], (K_MOVE, V_MOVE)),
        (r_att.at[pl.ds(0, 15 * 9)], (ATT_AR,)),
        (r_attn.at[pl.ds(0, 56)], (ATT_AG,)),
        (r_out.at[pl.ds(0, 7)], (OUT_AR,)),
        (r_ffn.at[pl.ds(0, 7)], (FFN_RS, FFN_AR)),
        (r_hid.at[pl.ds(0, 7)], (FFN_AG,)),
        (r_down.at[pl.ds(0, 7)], (DOWN_AR,)),
    )
    for ref, stages in sent:
        for stage in stages:
            pltpu.make_async_copy(ref, ref, send_sem.at[stage]).wait()
    arrived(r_down.at[pl.ds(0, 7)], DOWN_AR)
    layer = x_mid + total_of(r_down, pl.ds(0, 8))
    out_ref[2] = layer[0:4].astype(BF16)
    out_ref[3] = layer[4:8].astype(BF16)


def body(tokens, lengths, attn_gain, ffn_gain, w_q, w_k, w_v, w_o, w_gate, w_up, w_down, k_cache, v_cache):
    half = np.arange(64, dtype=np.float64)
    freq = np.tile(500000.0 ** (-2.0 * half / 128.0), 2).astype(np.float32)[None]
    k_cache = k_cache.reshape(4, 256, 128)
    v_cache = v_cache.reshape(4, 256, 128)
    hbm = pl.BlockSpec(memory_space=pltpu.HBM)
    small = (tokens, attn_gain.reshape(1, 128), ffn_gain.reshape(1, 128), jnp.asarray(freq))
    weights = (w_q, w_k, w_v, w_o, w_gate, w_up, w_down, k_cache, v_cache)
    both = pl.pallas_call(
        kernel,
        out_shape=pltpu.VMEM((4, 4, 128), BF16),
        in_specs=[hbm] * 14,
        out_specs=pl.BlockSpec(memory_space=pltpu.VMEM),
        scratch_shapes=[pltpu.SMEM((4,), jnp.int32)]
        + [pltpu.VMEM(a.shape, a.dtype) for a in small + weights]
        + [
            pltpu.VMEM((128, 128), F32), pltpu.VMEM((8, 16, 128), F32), pltpu.VMEM((16, 16, 128), F32),
            pltpu.VMEM((2, 16, 128), F32), pltpu.VMEM((256, 128), F32),
            pltpu.VMEM((64, 128), F32),
            pltpu.VMEM((8, 8, 128), F32),
            pltpu.VMEM((8, 16, BLOCK), BF16), pltpu.VMEM((8, 16, BLOCK), BF16), pltpu.VMEM((8, 16, BLOCK), BF16),
            pltpu.VMEM((8, 16, 256), BF16),
            pltpu.VMEM((8, 8, 128), F32),
            pltpu.SemaphoreType.DMA((14,)),
            pltpu.SemaphoreType.DMA((11,)),
            pltpu.SemaphoreType.DMA((11,)),
            pltpu.SemaphoreType.REGULAR((6,)),
        ],
        compiler_params=pltpu.CompilerParams(
            collective_id=0, has_side_effects=True, vmem_limit_bytes=60 * 1024 * 1024
        ),
    )(*[pltpu.with_memory_space_constraint(a, pltpu.HBM) for a in (lengths, *small, *weights)])
    return both[0:2], both[2:4]


def solution(mesh):
    return jax.shard_map(
        body,
        mesh=mesh,
        in_specs=(
            P(None, None, "ctx"),
            P(),
            P("ctx"),
            P("ctx"),
            P("ctx", "kvh"),
            P("ctx", "kvh"),
            P("ctx", "kvh"),
            P("kvh", "ctx"),
            P("ctx", "kvh"),
            P("ctx", "kvh"),
            P("kvh", "ctx"),
            P(None, "ctx", "kvh", None),
            P(None, "ctx", "kvh", None),
        ),
        out_specs=(P(None, None, "ctx"), P(None, None, "ctx")),
        check_vma=False,
    )
```

```python
import math

import jax
import jax.numpy as jnp
import numpy as np
from jax import lax
from jax.experimental import pallas as pl
from jax.experimental.pallas import tpu as pltpu
from jax.sharding import PartitionSpec as P

MESH = pl.DeviceIdType.MESH
D = 8192
EPS = 1e-05
F32 = jnp.float32
BF16 = jnp.bfloat16
FAR_FIRST = (4, 3, 5, 2, 6, 1, 7)
RING = ((2, 0), (2, 1), (1, 0), (3, 0), (1, 1), (3, 1), (0, 1))
TILES = 28
BLOCK = 512
QKV_RS, QKV_AR, K_MOVE, V_MOVE, ATT_AR, ATT_AG, OUT_AR, FFN_RS, FFN_AR, FFN_AG, DOWN_AR = range(11)


def total_of(ref, rows):
    parts = [ref[i, rows, :].astype(F32) for i in range(8)]
    return ((parts[0] + parts[1]) + (parts[2] + parts[3])) + (
        (parts[4] + parts[5]) + (parts[6] + parts[7])
    )


def column_of(line):
    lane = lax.broadcasted_iota(jnp.int32, (8, 128), 1)
    row = lax.broadcasted_iota(jnp.int32, (8, 128), 0)
    return jnp.sum(jnp.where(lane == row, line, 0.0), axis=1, keepdims=True)


def with_square(both, square, core):
    lane = lax.broadcasted_iota(jnp.int32, (16, 128), 1)
    high = square.astype(BF16).astype(F32)
    terms = jnp.concatenate([high, square - high], axis=0)
    first = jnp.where((core == 1) & (lane < 64), terms, both[:, 0:128])
    last = jnp.where((core == 0) & (lane >= 64), terms, both[:, 384:512])
    return jnp.concatenate([first, both[:, 128:384], last], axis=1)


def square_of(both, core):
    lane = lax.broadcasted_iota(jnp.int32, (16, 128), 1)
    tile = jnp.where(core == 1, both[:, 0:128], pltpu.roll(both[:, 384:512], 64, 1))
    tile = jnp.where(lane < 64, tile, pltpu.roll(tile, 64, 1))
    return tile[0:8] + tile[8:16]


def merged(ref):
    lines = ref[pl.ds(8, 16, stride=16), :]
    head = lax.broadcasted_iota(jnp.int32, (16, 128), 1) < 8
    peak = jnp.max(lines, axis=0, keepdims=True)
    factors = jnp.where(head, jnp.exp(jnp.where(head, lines - peak, 0.0)), 0.0)
    total = jnp.sum(factors * pltpu.roll(lines, 120, 1), axis=0, keepdims=True)
    terms = [column_of(factors[i : i + 1]) * ref[i * 16 : i * 16 + 8, :] for i in range(16)]
    while len(terms) > 1:
        terms = [a + b for a, b in zip(terms[0::2], terms[1::2])]
    return column_of(peak), column_of(total), terms[0]


def kernel(
    h_lengths, h_tokens, h_attn_gain, h_ffn_gain, h_freq,
    h_q, h_k, h_v, h_o, h_gate, h_up, h_down, h_kc, h_vc,
    out_ref,
    lengths, tokens, attn_gain, ffn_gain, freq,
    w_q, w_k, w_v, w_o, w_gate, w_up, w_down, k_c, v_c,
    s_qkv, r_qkv, r_qkv2,
    s_att, r_att, r_attn,
    r_out,
    s_ffn, r_ffn, r_ffn2, r_hid,
    r_down,
    load_sem, send_sem, recv_sem, near_sem,
):
    ctx = lax.axis_index("ctx")
    kvh = lax.axis_index("kvh")
    xc = lax.rem(ctx, 8)
    z = ctx // 8
    x = xc // 2
    c = lax.rem(xc, 2)

    def xc_peer(step):
        dx, dc = step
        to = lax.rem(x + dx, 4) * 2 + lax.rem(c + dc, 2)
        return to, (z * 8 + to, kvh)

    def z_peer(d):
        return (lax.rem(z + d, 8) * 8 + xc, kvh)

    def z_other(d):
        return (lax.rem(z + d, 8) * 8 + x * 2 + (1 - c), kvh)

    def y_peer(d):
        return (ctx, lax.rem(kvh + d, 8))

    def zc_peers():
        for d in FAR_FIRST:
            yield c, (lax.rem(z + d, 8) * 8 + xc, kvh)
            yield 1 - c, (lax.rem(z + d, 8) * 8 + x * 2 + (1 - c), kvh)
        yield 1 - c, (z * 8 + x * 2 + (1 - c), kvh)

    def send(src, dst, stage, peer):
        pltpu.make_async_remote_copy(
            src_ref=src, dst_ref=dst, send_sem=send_sem.at[stage], recv_sem=recv_sem.at[stage],
            device_id=peer, device_id_type=MESH,
        ).start()

    def arrived(ref, stage):
        pltpu.make_async_copy(ref, ref, recv_sem.at[stage]).wait()

    barrier = pltpu.get_barrier_semaphore()
    near = [z_peer(d) for d in (2, 6, 1, 7)] + [z_other(d) for d in (2, 6, 1, 7)] + [y_peer(1), y_peer(7)]
    for peer in near + [xc_peer(d)[1] for d in RING]:
        pl.semaphore_signal(barrier, inc=1, device_id=peer, device_id_type=MESH)

    def tell(i, peer_at, steps=(1, 7)):
        for d in steps:
            pl.semaphore_signal(near_sem.at[i], inc=1, device_id=peer_at(d), device_id_type=MESH)

    def heard(i, count=2):
        pl.semaphore_wait(near_sem.at[i], count)

    loads = {}
    for i, (name, src, dst) in enumerate(
        (
            ("tokens", h_tokens, tokens), ("attn_gain", h_attn_gain, attn_gain),
            ("q", h_q, w_q), ("k", h_k, w_k), ("v", h_v, w_v),
            ("lengths", h_lengths, lengths), ("freq", h_freq, freq), ("ffn_gain", h_ffn_gain, ffn_gain),
            ("kc", h_kc.at[x], k_c.at[x]), ("vc", h_vc.at[x], v_c.at[x]),
            ("o", h_o, w_o), ("gate", h_gate, w_gate), ("up", h_up, w_up), ("down", h_down, w_down),
        )
    ):
        loads[name] = pltpu.make_async_copy(src, dst, load_sem.at[i])
        loads[name].start()
    loads["tokens"].wait()
    loads["attn_gain"].wait()
    hid = jnp.concatenate([tokens[0], tokens[1]], axis=0).astype(F32)
    sq = jnp.broadcast_to(jnp.sum(hid * hid, axis=1, keepdims=True), (8, 128))
    xg = (hid * attn_gain[...].astype(F32)).astype(BF16)
    for name in ("q", "k", "v"):
        loads[name].wait()
    q_part = jnp.dot(xg, w_q[...], preferred_element_type=F32)
    k_part = jnp.dot(xg, w_k[...], preferred_element_type=F32)
    v_part = jnp.dot(xg, w_v[...], preferred_element_type=F32)
    for h in range(8):
        s_qkv[pl.ds(h, 8, stride=16), :] = q_part[:, h * 128 : (h + 1) * 128]
    s_qkv[pl.ds(8, 8, stride=16), :] = k_part
    s_qkv[pl.ds(9, 8, stride=16), :] = v_part
    s_qkv[pl.ds(10, 8, stride=16), :] = sq

    def row_block(to):
        return pl.ds(pl.multiple_of((lax.rem(to, 2) * 4 + to // 2) * 16, 16), 11)

    r_qkv[xc, 0:11, :] = s_qkv[row_block(xc), :]

    pl.semaphore_wait(barrier, 17)
    tell(0, z_peer, (2, 6, 1, 7))
    for d in RING:
        to, peer = xc_peer(d)
        send(s_qkv.at[row_block(to)], r_qkv.at[xc, pl.ds(0, 11)], QKV_RS, peer)
    for d in (2, 1, 3):
        to = lax.rem(x + d, 4)
        peer = (z * 8 + to * 2 + c, kvh)
        send(h_kc.at[to], k_c.at[x], K_MOVE, peer)

    heard(0, 4)

    loads["lengths"].wait()
    loads["freq"].wait()
    step8 = lax.broadcasted_iota(jnp.int32, (8, 128), 0)
    lane = lax.broadcasted_iota(jnp.int32, (8, 128), 1)
    length = lengths[x]
    angle = (length + step8).astype(F32) * freq[...]
    cosine = jnp.cos(angle)
    sine = jnp.sin(angle)
    sine = jnp.where(lane < 64, -sine, sine)

    tell(3, y_peer)
    arrived(r_qkv.at[pl.ds(0, 7), pl.ds(0, 11)], QKV_RS)
    r_qkv2[z * 2 + c, 0:11, :] = total_of(r_qkv, pl.ds(0, 11))
    mine = r_qkv2.at[z * 2 + c, pl.ds(0, 11)]
    for _, peer in zc_peers():
        send(mine, mine, QKV_AR, peer)
    for d in (2, 1, 3):
        to = lax.rem(x + d, 4)
        send(h_vc.at[to], v_c.at[x], V_MOVE, (z * 8 + to * 2 + c, kvh))
    heard(3)
    tell(4, y_peer)
    arrived(r_qkv2.at[pl.ds(0, 15), pl.ds(0, 11)], QKV_AR)
    queries, new_keys, new_values = [], [], []
    for s in range(2):
        parts = [r_qkv2[i * 2 + s, 0:11, :] for i in range(8)]
        while len(parts) > 1:
            parts = [a + b for a, b in zip(parts[0::2], parts[1::2])]
        whole = parts[0]
        scale = lax.rsqrt(whole[10:11] / D + EPS)

        def rotary(a):
            return a * cosine[s : s + 1] + pltpu.roll(a, 64, 1) * sine[s : s + 1]

        queries.append(rotary(whole[0:8] * scale).astype(BF16))
        key = jnp.broadcast_to(whole[8:9] * scale, (8, 128))
        new_keys.append(rotary(key).astype(BF16).astype(F32))
        value = jnp.broadcast_to(whole[9:10] * scale, (8, 128))
        new_values.append(value.astype(BF16).astype(F32))
    both_steps = jnp.concatenate(queries, axis=0)
    loads["kc"].wait()
    loads["vc"].wait()
    arrived(k_c.at[pl.ds(0, 3)], K_MOVE)

    scores, valid = [], []
    for i in range(4):
        scores.append(
            lax.dot_general(both_steps, k_c[i], (((1,), (1,)), ((), ())), preferred_element_type=F32)
            / math.sqrt(128)
        )
        first = (z * 8 + i * 2 + c) * 256
        valid.append(first + lax.broadcasted_iota(jnp.int32, (16, 256), 1) < length)
    scores = jnp.concatenate(scores, axis=1)
    valid = jnp.concatenate(valid, axis=1)
    scores = jnp.where(valid, scores, -1e30)
    peak = jnp.max(scores, axis=1, keepdims=True)
    weights = jnp.where(valid, jnp.exp(scores - peak), 0.0)
    total = jnp.sum(weights, axis=1, keepdims=True)
    weights = weights.astype(BF16)
    arrived(v_c.at[pl.ds(0, 3)], V_MOVE)
    acc = jnp.zeros((16, 128), F32)
    for i in range(4):
        acc += jnp.dot(weights[:, i * 256 : (i + 1) * 256], v_c[i], preferred_element_type=F32)
    for s in range(2):
        rows = slice(s * 8, s * 8 + 8)
        s_att[s, 0:8, :] = acc[rows]
        line = jnp.where(lane == step8, peak[rows], jnp.where(lane == step8 + 8, total[rows], 0.0))
        s_att[s, 8:9, :] = jnp.sum(line, axis=0, keepdims=True)
    slot = pl.ds(pl.multiple_of((z * 2 + c) * 16, 16), 9)
    r_att[slot, :] = s_att[c, 0:9, :]
    for core, peer in zc_peers():
        send(s_att.at[core, pl.ds(0, 9)], r_att.at[slot], ATT_AR, peer)

    q_mine = jnp.where(c == 0, queries[0].astype(F32), queries[1].astype(F32))
    fresh = [jnp.sum(q_mine * key, axis=1, keepdims=True) / math.sqrt(128) for key in new_keys]
    f_first = jnp.broadcast_to(fresh[0], (8, 128))
    f_second = jnp.where(c == 1, jnp.broadcast_to(fresh[1], (8, 128)), -1e30)

    heard(4)
    tell(5, y_peer)
    heard(5)
    loads["o"].wait()
    arrived(r_att.at[pl.ds(0, 15 * 9)], ATT_AR)
    peak, total, summed = merged(r_att)
    top = jnp.maximum(peak, jnp.maximum(f_first, f_second))
    factor = jnp.exp(peak - top)
    e_first = jnp.exp(f_first - top)
    e_second = jnp.where(c == 1, jnp.exp(f_second - top), 0.0)
    total = total * factor + e_first + e_second
    summed = (
        summed * factor
        + e_first.astype(BF16).astype(F32) * new_values[0]
        + e_second.astype(BF16).astype(F32) * new_values[1]
    )
    mine = r_attn.at[pl.ds(pl.multiple_of((c * 4 + x) * 8, 8), 8)]
    mine[...] = summed / total
    for d in RING:
        send(mine, mine, ATT_AG, xc_peer(d)[1])
    arrived(r_attn.at[pl.ds(0, 56)], ATT_AG)

    attn = jnp.concatenate([r_attn[pl.ds(h, 8, stride=8), :] for h in range(8)], axis=1).astype(BF16)
    r_out[kvh] = jnp.dot(attn, w_o[...], preferred_element_type=F32)
    for d in FAR_FIRST:
        send(r_out.at[kvh], r_out.at[kvh], OUT_AR, y_peer(d))
    for name in ("gate", "up", "ffn_gain"):
        loads[name].wait()
    arrived(r_out.at[pl.ds(0, 7)], OUT_AR)
    attended = total_of(r_out, pl.ds(0, 8))
    x_mid = hid + attended
    square = jnp.broadcast_to(jnp.sum(x_mid * x_mid, axis=1, keepdims=True), (8, 128))

    xh = (x_mid * ffn_gain[...].astype(F32)).astype(BF16)
    for d in RING + ((0, 0),):
        to, peer = xc_peer(d)
        start = pl.multiple_of(((to // 2) * 7 + lax.rem(to, 2) * 3) * 128, 128)
        gate = jnp.dot(xh, w_gate[:, pl.ds(start, BLOCK)], preferred_element_type=F32)
        up = jnp.dot(xh, w_up[:, pl.ds(start, BLOCK)], preferred_element_type=F32)
        both = with_square(jnp.concatenate([gate, up], axis=0), square, lax.rem(to, 2)).astype(BF16)
        if d != (0, 0):
            s_ffn[to] = both
            send(s_ffn.at[to], r_ffn.at[xc], FFN_RS, peer)
        else:
            r_ffn[xc] = both
    out_ref[0] = attended[0:4].astype(BF16)
    out_ref[1] = attended[4:8].astype(BF16)
    arrived(r_ffn.at[pl.ds(0, 7)], FFN_RS)
    both = total_of(r_ffn, pl.ds(0, 16))
    r_ffn2[z] = with_square(both, square_of(both, c), c).astype(BF16)
    for d in FAR_FIRST:
        send(r_ffn2.at[z], r_ffn2.at[z], FFN_AR, z_peer(d))
    loads["down"].wait()
    arrived(r_ffn2.at[pl.ds(0, 7)], FFN_AR)
    both = total_of(r_ffn2, pl.ds(0, 16))
    scale = lax.rsqrt(square_of(both, c) / D + EPS)[:, 0:1]
    gate = both[0:8] * scale
    hidden = gate / (1.0 + jnp.exp(-gate)) * (both[8:16] * scale)
    unit = lax.broadcasted_iota(jnp.int32, (8, BLOCK), 1)
    hidden = jnp.where((unit >= c * 64) & (unit < 448 + c * 64), hidden, 0.0)
    r_hid[xc] = jnp.concatenate([hidden[:, 0:256], hidden[:, 256:512]], axis=0).astype(BF16)
    for d in RING:
        send(r_hid.at[xc], r_hid.at[xc], FFN_AG, xc_peer(d)[1])
    arrived(r_hid.at[pl.ds(0, 7)], FFN_AG)

    pieces = []
    for j in range(4):
        even = r_hid[2 * j].astype(F32)
        odd = r_hid[2 * j + 1].astype(F32)
        pieces += [
            even[0:8], even[8:16, 0:128], even[8:16, 128:256] + odd[0:8, 0:128], odd[0:8, 128:256], odd[8:16]
        ]
    r_down[kvh] = jnp.dot(
        jnp.concatenate(pieces, axis=1).astype(BF16), w_down[...], preferred_element_type=F32
    )
    for d in FAR_FIRST:
        send(r_down.at[kvh], r_down.at[kvh], DOWN_AR, y_peer(d))
    sent = (
        (r_qkv.at[pl.ds(0, 7), pl.ds(0, 11)], (QKV_RS,)),
        (r_qkv2.at[pl.ds(0, 15), pl.ds(0, 11)], (QKV_AR,)),
        (k_c.at[pl.ds(0, 3)], (K_MOVE, V_MOVE)),
        (r_att.at[pl.ds(0, 15 * 9)], (ATT_AR,)),
        (r_attn.at[pl.ds(0, 56)], (ATT_AG,)),
        (r_out.at[pl.ds(0, 7)], (OUT_AR,)),
        (r_ffn.at[pl.ds(0, 7)], (FFN_RS, FFN_AR)),
        (r_hid.at[pl.ds(0, 7)], (FFN_AG,)),
        (r_down.at[pl.ds(0, 7)], (DOWN_AR,)),
    )
    for ref, stages in sent:
        for stage in stages:
            pltpu.make_async_copy(ref, ref, send_sem.at[stage]).wait()
    arrived(r_down.at[pl.ds(0, 7)], DOWN_AR)
    layer = x_mid + total_of(r_down, pl.ds(0, 8))
    out_ref[2] = layer[0:4].astype(BF16)
    out_ref[3] = layer[4:8].astype(BF16)


def body(tokens, lengths, attn_gain, ffn_gain, w_q, w_k, w_v, w_o, w_gate, w_up, w_down, k_cache, v_cache):
    half = np.arange(64, dtype=np.float64)
    freq = np.tile(500000.0 ** (-2.0 * half / 128.0), 2).astype(np.float32)[None]
    k_cache = k_cache.reshape(4, 256, 128)
    v_cache = v_cache.reshape(4, 256, 128)
    hbm = pl.BlockSpec(memory_space=pltpu.HBM)
    small = (tokens, attn_gain.reshape(1, 128), ffn_gain.reshape(1, 128), jnp.asarray(freq))
    weights = (w_q, w_k, w_v, w_o, w_gate, w_up, w_down, k_cache, v_cache)
    both = pl.pallas_call(
        kernel,
        out_shape=pltpu.VMEM((4, 4, 128), BF16),
        in_specs=[hbm] * 14,
        out_specs=pl.BlockSpec(memory_space=pltpu.VMEM),
        scratch_shapes=[pltpu.SMEM((4,), jnp.int32)]
        + [pltpu.VMEM(a.shape, a.dtype) for a in small + weights]
        + [
            pltpu.VMEM((128, 128), F32), pltpu.VMEM((8, 16, 128), F32), pltpu.VMEM((16, 16, 128), F32),
            pltpu.VMEM((2, 16, 128), F32), pltpu.VMEM((256, 128), F32),
            pltpu.VMEM((64, 128), F32),
            pltpu.VMEM((8, 8, 128), F32),
            pltpu.VMEM((8, 16, BLOCK), BF16), pltpu.VMEM((8, 16, BLOCK), BF16), pltpu.VMEM((8, 16, BLOCK), BF16),
            pltpu.VMEM((8, 16, 256), BF16),
            pltpu.VMEM((8, 8, 128), F32),
            pltpu.SemaphoreType.DMA((14,)),
            pltpu.SemaphoreType.DMA((11,)),
            pltpu.SemaphoreType.DMA((11,)),
            pltpu.SemaphoreType.REGULAR((6,)),
        ],
        compiler_params=pltpu.CompilerParams(
            collective_id=0, has_side_effects=True, vmem_limit_bytes=60 * 1024 * 1024
        ),
    )(*[pltpu.with_memory_space_constraint(a, pltpu.HBM) for a in (lengths, *small, *weights)])
    return both[0:2], both[2:4]


def solution(mesh):
    return jax.shard_map(
        body,
        mesh=mesh,
        in_specs=(
            P(None, None, "ctx"),
            P(),
            P("ctx"),
            P("ctx"),
            P("ctx", "kvh"),
            P("ctx", "kvh"),
            P("ctx", "kvh"),
            P("kvh", "ctx"),
            P("ctx", "kvh"),
            P("ctx", "kvh"),
            P("kvh", "ctx"),
            P(None, "ctx", "kvh", None),
            P(None, "ctx", "kvh", None),
        ),
        out_specs=(P(None, None, "ctx"), P(None, None, "ctx")),
        check_vma=False,
    )
```

```python
import math

import jax
import jax.numpy as jnp
import numpy as np
from jax import lax
from jax.experimental import pallas as pl
from jax.experimental.pallas import tpu as pltpu
from jax.sharding import PartitionSpec as P

MESH = pl.DeviceIdType.MESH
D = 8192
EPS = 1e-05
F32 = jnp.float32
BF16 = jnp.bfloat16
FAR_FIRST = (4, 3, 5, 2, 6, 1, 7)
RING = ((2, 0), (2, 1), (1, 0), (3, 0), (1, 1), (3, 1), (0, 1))
TILES = 28
BLOCK = 512
QKV_RS, QKV_AR, K_MOVE, V_MOVE, ATT_AR, ATT_AG, OUT_AR, FFN_RS, FFN_AR, FFN_AG, DOWN_AR = range(11)


def total_of(ref, rows):
    parts = [ref[i, rows, :].astype(F32) for i in range(8)]
    return ((parts[0] + parts[1]) + (parts[2] + parts[3])) + (
        (parts[4] + parts[5]) + (parts[6] + parts[7])
    )


def column_of(line):
    lane = lax.broadcasted_iota(jnp.int32, (8, 128), 1)
    row = lax.broadcasted_iota(jnp.int32, (8, 128), 0)
    return jnp.sum(jnp.where(lane == row, line, 0.0), axis=1, keepdims=True)


def with_square(both, square, core):
    lane = lax.broadcasted_iota(jnp.int32, (16, 128), 1)
    high = square.astype(BF16).astype(F32)
    terms = jnp.concatenate([high, square - high], axis=0)
    first = jnp.where((core == 1) & (lane < 64), terms, both[:, 0:128])
    last = jnp.where((core == 0) & (lane >= 64), terms, both[:, 384:512])
    return jnp.concatenate([first, both[:, 128:384], last], axis=1)


def square_of(both, core):
    lane = lax.broadcasted_iota(jnp.int32, (16, 128), 1)
    tile = jnp.where(core == 1, both[:, 0:128], pltpu.roll(both[:, 384:512], 64, 1))
    tile = jnp.where(lane < 64, tile, pltpu.roll(tile, 64, 1))
    return tile[0:8] + tile[8:16]


def merged(ref):
    lines = ref[pl.ds(8, 16, stride=16), :]
    head = lax.broadcasted_iota(jnp.int32, (16, 128), 1) < 8
    peak = jnp.max(lines, axis=0, keepdims=True)
    factors = jnp.where(head, jnp.exp(jnp.where(head, lines - peak, 0.0)), 0.0)
    total = jnp.sum(factors * pltpu.roll(lines, 120, 1), axis=0, keepdims=True)
    terms = [column_of(factors[i : i + 1]) * ref[i * 16 : i * 16 + 8, :] for i in range(16)]
    while len(terms) > 1:
        terms = [a + b for a, b in zip(terms[0::2], terms[1::2])]
    return column_of(peak), column_of(total), terms[0]


def kernel(
    h_lengths, h_tokens, h_attn_gain, h_ffn_gain, h_freq,
    h_q, h_k, h_v, h_o, h_gate, h_up, h_down, h_kc, h_vc,
    out_ref,
    lengths, tokens, attn_gain, ffn_gain, freq,
    w_q, w_k, w_v, w_o, w_gate, w_up, w_down, k_c, v_c,
    s_qkv, r_qkv, r_qkv2,
    s_att, r_att, r_attn,
    r_out,
    s_ffn, r_ffn, r_ffn2, r_hid,
    r_down,
    load_sem, send_sem, recv_sem, near_sem,
):
    ctx = lax.axis_index("ctx")
    kvh = lax.axis_index("kvh")
    xc = lax.rem(ctx, 8)
    z = ctx // 8
    x = xc // 2
    c = lax.rem(xc, 2)

    def xc_peer(step):
        dx, dc = step
        to = lax.rem(x + dx, 4) * 2 + lax.rem(c + dc, 2)
        return to, (z * 8 + to, kvh)

    def z_peer(d):
        return (lax.rem(z + d, 8) * 8 + xc, kvh)

    def z_other(d):
        return (lax.rem(z + d, 8) * 8 + x * 2 + (1 - c), kvh)

    def y_peer(d):
        return (ctx, lax.rem(kvh + d, 8))

    def zc_peers():
        for d in FAR_FIRST:
            yield c, (lax.rem(z + d, 8) * 8 + xc, kvh)
            yield 1 - c, (lax.rem(z + d, 8) * 8 + x * 2 + (1 - c), kvh)
        yield 1 - c, (z * 8 + x * 2 + (1 - c), kvh)

    def send(src, dst, stage, peer):
        pltpu.make_async_remote_copy(
            src_ref=src, dst_ref=dst, send_sem=send_sem.at[stage], recv_sem=recv_sem.at[stage],
            device_id=peer, device_id_type=MESH,
        ).start()

    def arrived(ref, stage):
        pltpu.make_async_copy(ref, ref, recv_sem.at[stage]).wait()

    barrier = pltpu.get_barrier_semaphore()
    near = [z_peer(d) for d in (2, 6, 1, 7)] + [z_other(d) for d in (2, 6, 1, 7)] + [y_peer(1), y_peer(7)]
    for peer in near + [xc_peer(d)[1] for d in RING]:
        pl.semaphore_signal(barrier, inc=1, device_id=peer, device_id_type=MESH)

    def tell(i, peer_at, steps=(1, 7)):
        for d in steps:
            pl.semaphore_signal(near_sem.at[i], inc=1, device_id=peer_at(d), device_id_type=MESH)

    def heard(i, count=2):
        pl.semaphore_wait(near_sem.at[i], count)

    loads = {}
    for i, (name, src, dst) in enumerate(
        (
            ("tokens", h_tokens, tokens), ("attn_gain", h_attn_gain, attn_gain),
            ("q", h_q, w_q), ("k", h_k, w_k), ("v", h_v, w_v),
            ("lengths", h_lengths, lengths), ("freq", h_freq, freq), ("ffn_gain", h_ffn_gain, ffn_gain),
            ("kc", h_kc.at[x], k_c.at[x]), ("vc", h_vc.at[x], v_c.at[x]),
            ("o", h_o, w_o), ("gate", h_gate, w_gate), ("up", h_up, w_up), ("down", h_down, w_down),
        )
    ):
        loads[name] = pltpu.make_async_copy(src, dst, load_sem.at[i])
        loads[name].start()
    loads["tokens"].wait()
    loads["attn_gain"].wait()
    hid = jnp.concatenate([tokens[0], tokens[1]], axis=0).astype(F32)
    sq = jnp.broadcast_to(jnp.sum(hid * hid, axis=1, keepdims=True), (8, 128))
    xg = (hid * attn_gain[...].astype(F32)).astype(BF16)
    for name in ("q", "k", "v"):
        loads[name].wait()
    q_part = jnp.dot(xg, w_q[...], preferred_element_type=F32)
    k_part = jnp.dot(xg, w_k[...], preferred_element_type=F32)
    v_part = jnp.dot(xg, w_v[...], preferred_element_type=F32)
    for h in range(8):
        s_qkv[pl.ds(h, 8, stride=16), :] = q_part[:, h * 128 : (h + 1) * 128]
    s_qkv[pl.ds(8, 8, stride=16), :] = k_part
    s_qkv[pl.ds(9, 8, stride=16), :] = v_part
    s_qkv[pl.ds(10, 8, stride=16), :] = sq

    def row_block(to):
        return pl.ds(pl.multiple_of((lax.rem(to, 2) * 4 + to // 2) * 16, 16), 11)

    r_qkv[xc, 0:11, :] = s_qkv[row_block(xc), :]

    pl.semaphore_wait(barrier, 17)
    tell(0, z_peer, (2, 6, 1, 7))
    for d in RING:
        to, peer = xc_peer(d)
        send(s_qkv.at[row_block(to)], r_qkv.at[xc, pl.ds(0, 11)], QKV_RS, peer)
    for d in (2, 1, 3):
        to = lax.rem(x + d, 4)
        peer = (z * 8 + to * 2 + c, kvh)
        send(h_kc.at[to], k_c.at[x], K_MOVE, peer)

    heard(0, 4)

    loads["lengths"].wait()
    loads["freq"].wait()
    step8 = lax.broadcasted_iota(jnp.int32, (8, 128), 0)
    lane = lax.broadcasted_iota(jnp.int32, (8, 128), 1)
    length = lengths[x]
    angle = (length + step8).astype(F32) * freq[...]
    cosine = jnp.cos(angle)
    sine = jnp.sin(angle)
    sine = jnp.where(lane < 64, -sine, sine)

    tell(3, y_peer)
    arrived(r_qkv.at[pl.ds(0, 7), pl.ds(0, 11)], QKV_RS)
    r_qkv2[z * 2 + c, 0:11, :] = total_of(r_qkv, pl.ds(0, 11))
    mine = r_qkv2.at[z * 2 + c, pl.ds(0, 11)]
    for _, peer in zc_peers():
        send(mine, mine, QKV_AR, peer)
    for d in (2, 1, 3):
        to = lax.rem(x + d, 4)
        send(h_vc.at[to], v_c.at[x], V_MOVE, (z * 8 + to * 2 + c, kvh))
    heard(3)
    tell(4, y_peer)
    arrived(r_qkv2.at[pl.ds(0, 15), pl.ds(0, 11)], QKV_AR)
    queries, new_keys, new_values = [], [], []
    for s in range(2):
        parts = [r_qkv2[i * 2 + s, 0:11, :] for i in range(8)]
        while len(parts) > 1:
            parts = [a + b for a, b in zip(parts[0::2], parts[1::2])]
        whole = parts[0]
        scale = lax.rsqrt(whole[10:11] / D + EPS)

        def rotary(a):
            return a * cosine[s : s + 1] + pltpu.roll(a, 64, 1) * sine[s : s + 1]

        queries.append(rotary(whole[0:8] * scale).astype(BF16))
        key = jnp.broadcast_to(whole[8:9] * scale, (8, 128))
        new_keys.append(rotary(key).astype(BF16).astype(F32))
        value = jnp.broadcast_to(whole[9:10] * scale, (8, 128))
        new_values.append(value.astype(BF16).astype(F32))
    both_steps = jnp.concatenate(queries, axis=0)
    loads["kc"].wait()
    loads["vc"].wait()
    arrived(k_c.at[pl.ds(0, 3)], K_MOVE)

    scores, valid = [], []
    for i in range(4):
        scores.append(
            lax.dot_general(both_steps, k_c[i], (((1,), (1,)), ((), ())), preferred_element_type=F32)
            / math.sqrt(128)
        )
        first = (z * 8 + i * 2 + c) * 256
        valid.append(first + lax.broadcasted_iota(jnp.int32, (16, 256), 1) < length)
    scores = jnp.concatenate(scores, axis=1)
    valid = jnp.concatenate(valid, axis=1)
    scores = jnp.where(valid, scores, -1e30)
    peak = jnp.max(scores, axis=1, keepdims=True)
    weights = jnp.where(valid, jnp.exp(scores - peak), 0.0)
    total = jnp.sum(weights, axis=1, keepdims=True)
    weights = weights.astype(BF16)
    arrived(v_c.at[pl.ds(0, 3)], V_MOVE)
    acc = jnp.zeros((16, 128), F32)
    for i in range(4):
        acc += jnp.dot(weights[:, i * 256 : (i + 1) * 256], v_c[i], preferred_element_type=F32)
    for s in range(2):
        rows = slice(s * 8, s * 8 + 8)
        s_att[s, 0:8, :] = acc[rows]
        line = jnp.where(lane == step8, peak[rows], jnp.where(lane == step8 + 8, total[rows], 0.0))
        s_att[s, 8:9, :] = jnp.sum(line, axis=0, keepdims=True)
    slot = pl.ds(pl.multiple_of((z * 2 + c) * 16, 16), 9)
    r_att[slot, :] = s_att[c, 0:9, :]
    for core, peer in zc_peers():
        send(s_att.at[core, pl.ds(0, 9)], r_att.at[slot], ATT_AR, peer)

    q_mine = jnp.where(c == 0, queries[0].astype(F32), queries[1].astype(F32))
    fresh = [jnp.sum(q_mine * key, axis=1, keepdims=True) / math.sqrt(128) for key in new_keys]
    f_first = jnp.broadcast_to(fresh[0], (8, 128))
    f_second = jnp.where(c == 1, jnp.broadcast_to(fresh[1], (8, 128)), -1e30)

    heard(4)
    tell(5, y_peer)
    heard(5)
    loads["o"].wait()
    arrived(r_att.at[pl.ds(0, 15 * 9)], ATT_AR)
    peak, total, summed = merged(r_att)
    top = jnp.maximum(peak, jnp.maximum(f_first, f_second))
    factor = jnp.exp(peak - top)
    e_first = jnp.exp(f_first - top)
    e_second = jnp.where(c == 1, jnp.exp(f_second - top), 0.0)
    total = total * factor + e_first + e_second
    summed = (
        summed * factor
        + e_first.astype(BF16).astype(F32) * new_values[0]
        + e_second.astype(BF16).astype(F32) * new_values[1]
    )
    mine = r_attn.at[pl.ds(pl.multiple_of((c * 4 + x) * 8, 8), 8)]
    mine[...] = summed / total
    for d in RING:
        send(mine, mine, ATT_AG, xc_peer(d)[1])
    arrived(r_attn.at[pl.ds(0, 56)], ATT_AG)

    attn = jnp.concatenate([r_attn[pl.ds(h, 8, stride=8), :] for h in range(8)], axis=1).astype(BF16)
    r_out[kvh] = jnp.dot(attn, w_o[...], preferred_element_type=F32)
    for d in FAR_FIRST:
        send(r_out.at[kvh], r_out.at[kvh], OUT_AR, y_peer(d))
    for name in ("gate", "up", "ffn_gain"):
        loads[name].wait()
    arrived(r_out.at[pl.ds(0, 7)], OUT_AR)
    attended = total_of(r_out, pl.ds(0, 8))
    x_mid = hid + attended
    square = jnp.broadcast_to(jnp.sum(x_mid * x_mid, axis=1, keepdims=True), (8, 128))

    xh = (x_mid * ffn_gain[...].astype(F32)).astype(BF16)
    for d in RING + ((0, 0),):
        to, peer = xc_peer(d)
        start = pl.multiple_of(((to // 2) * 7 + lax.rem(to, 2) * 3) * 128, 128)
        gate = jnp.dot(xh, w_gate[:, pl.ds(start, BLOCK)], preferred_element_type=F32)
        up = jnp.dot(xh, w_up[:, pl.ds(start, BLOCK)], preferred_element_type=F32)
        both = with_square(jnp.concatenate([gate, up], axis=0), square, lax.rem(to, 2)).astype(BF16)
        if d != (0, 0):
            s_ffn[to] = both
            send(s_ffn.at[to], r_ffn.at[xc], FFN_RS, peer)
        else:
            r_ffn[xc] = both
    out_ref[0] = attended[0:4].astype(BF16)
    out_ref[1] = attended[4:8].astype(BF16)
    arrived(r_ffn.at[pl.ds(0, 7)], FFN_RS)
    both = total_of(r_ffn, pl.ds(0, 16))
    r_ffn2[z] = with_square(both, square_of(both, c), c).astype(BF16)
    for d in FAR_FIRST:
        send(r_ffn2.at[z], r_ffn2.at[z], FFN_AR, z_peer(d))
    loads["down"].wait()
    arrived(r_ffn2.at[pl.ds(0, 7)], FFN_AR)
    both = total_of(r_ffn2, pl.ds(0, 16))
    scale = lax.rsqrt(square_of(both, c) / D + EPS)[:, 0:1]
    gate = both[0:8] * scale
    hidden = gate / (1.0 + jnp.exp(-gate)) * (both[8:16] * scale)
    unit = lax.broadcasted_iota(jnp.int32, (8, BLOCK), 1)
    hidden = jnp.where((unit >= c * 64) & (unit < 448 + c * 64), hidden, 0.0)
    r_hid[xc] = jnp.concatenate([hidden[:, 0:256], hidden[:, 256:512]], axis=0).astype(BF16)
    for d in RING:
        send(r_hid.at[xc], r_hid.at[xc], FFN_AG, xc_peer(d)[1])
    arrived(r_hid.at[pl.ds(0, 7)], FFN_AG)

    pieces = []
    for j in range(4):
        even = r_hid[2 * j].astype(F32)
        odd = r_hid[2 * j + 1].astype(F32)
        pieces += [
            even[0:8], even[8:16, 0:128], even[8:16, 128:256] + odd[0:8, 0:128], odd[0:8, 128:256], odd[8:16]
        ]
    r_down[kvh] = jnp.dot(
        jnp.concatenate(pieces, axis=1).astype(BF16), w_down[...], preferred_element_type=F32
    )
    for d in FAR_FIRST:
        send(r_down.at[kvh], r_down.at[kvh], DOWN_AR, y_peer(d))
    sent = (
        (r_qkv.at[pl.ds(0, 7), pl.ds(0, 11)], (QKV_RS,)),
        (r_qkv2.at[pl.ds(0, 15), pl.ds(0, 11)], (QKV_AR,)),
        (k_c.at[pl.ds(0, 3)], (K_MOVE, V_MOVE)),
        (r_att.at[pl.ds(0, 15 * 9)], (ATT_AR,)),
        (r_attn.at[pl.ds(0, 56)], (ATT_AG,)),
        (r_out.at[pl.ds(0, 7)], (OUT_AR,)),
        (r_ffn.at[pl.ds(0, 7)], (FFN_RS, FFN_AR)),
        (r_hid.at[pl.ds(0, 7)], (FFN_AG,)),
        (r_down.at[pl.ds(0, 7)], (DOWN_AR,)),
    )
    for ref, stages in sent:
        for stage in stages:
            pltpu.make_async_copy(ref, ref, send_sem.at[stage]).wait()
    arrived(r_down.at[pl.ds(0, 7)], DOWN_AR)
    layer = x_mid + total_of(r_down, pl.ds(0, 8))
    out_ref[2] = layer[0:4].astype(BF16)
    out_ref[3] = layer[4:8].astype(BF16)


def body(tokens, lengths, attn_gain, ffn_gain, w_q, w_k, w_v, w_o, w_gate, w_up, w_down, k_cache, v_cache):
    half = np.arange(64, dtype=np.float64)
    freq = np.tile(500000.0 ** (-2.0 * half / 128.0), 2).astype(np.float32)[None]
    k_cache = k_cache.reshape(4, 256, 128)
    v_cache = v_cache.reshape(4, 256, 128)
    hbm = pl.BlockSpec(memory_space=pltpu.HBM)
    small = (tokens, attn_gain.reshape(1, 128), ffn_gain.reshape(1, 128), jnp.asarray(freq))
    weights = (w_q, w_k, w_v, w_o, w_gate, w_up, w_down, k_cache, v_cache)
    both = pl.pallas_call(
        kernel,
        out_shape=pltpu.VMEM((4, 4, 128), BF16),
        in_specs=[hbm] * 14,
        out_specs=pl.BlockSpec(memory_space=pltpu.VMEM),
        scratch_shapes=[pltpu.SMEM((4,), jnp.int32)]
        + [pltpu.VMEM(a.shape, a.dtype) for a in small + weights]
        + [
            pltpu.VMEM((144, 128), F32), pltpu.VMEM((8, 16, 128), F32), pltpu.VMEM((16, 16, 128), F32),
            pltpu.VMEM((2, 16, 128), F32), pltpu.VMEM((272, 128), F32),
            pltpu.VMEM((72, 128), F32),
            pltpu.VMEM((8, 8, 128), F32),
            pltpu.VMEM((8, 16, BLOCK), BF16), pltpu.VMEM((8, 16, BLOCK), BF16), pltpu.VMEM((8, 16, BLOCK), BF16),
            pltpu.VMEM((8, 16, 256), BF16),
            pltpu.VMEM((8, 8, 128), F32),
            pltpu.SemaphoreType.DMA((14,)),
            pltpu.SemaphoreType.DMA((11,)),
            pltpu.SemaphoreType.DMA((11,)),
            pltpu.SemaphoreType.REGULAR((6,)),
        ],
        compiler_params=pltpu.CompilerParams(
            collective_id=0, has_side_effects=True, vmem_limit_bytes=60 * 1024 * 1024
        ),
    )(*[pltpu.with_memory_space_constraint(a, pltpu.HBM) for a in (lengths, *small, *weights)])
    return both[0:2], both[2:4]


def solution(mesh):
    return jax.shard_map(
        body,
        mesh=mesh,
        in_specs=(
            P(None, None, "ctx"),
            P(),
            P("ctx"),
            P("ctx"),
            P("ctx", "kvh"),
            P("ctx", "kvh"),
            P("ctx", "kvh"),
            P("kvh", "ctx"),
            P("ctx", "kvh"),
            P("ctx", "kvh"),
            P("kvh", "ctx"),
            P(None, "ctx", "kvh", None),
            P(None, "ctx", "kvh", None),
        ),
        out_specs=(P(None, None, "ctx"), P(None, None, "ctx")),
        check_vma=False,
    )
```

```python
import math

import jax
import jax.numpy as jnp
import numpy as np
from jax import lax
from jax.experimental import pallas as pl
from jax.experimental.pallas import tpu as pltpu
from jax.sharding import PartitionSpec as P

MESH = pl.DeviceIdType.MESH
D = 8192
EPS = 1e-05
F32 = jnp.float32
BF16 = jnp.bfloat16
FAR_FIRST = (4, 3, 5, 2, 6, 1, 7)
RING = ((2, 0), (2, 1), (1, 0), (3, 0), (1, 1), (3, 1), (0, 1))
TILES = 28
BLOCK = 512
QKV_RS, QKV_AR, K_MOVE, V_MOVE, ATT_AR, ATT_AG, OUT_AR, FFN_RS, FFN_AR, FFN_AG, DOWN_AR = range(11)


def total_of(ref, rows):
    parts = [ref[i, rows, :].astype(F32) for i in range(8)]
    return ((parts[0] + parts[1]) + (parts[2] + parts[3])) + (
        (parts[4] + parts[5]) + (parts[6] + parts[7])
    )


def column_of(line):
    lane = lax.broadcasted_iota(jnp.int32, (8, 128), 1)
    row = lax.broadcasted_iota(jnp.int32, (8, 128), 0)
    return jnp.sum(jnp.where(lane == row, line, 0.0), axis=1, keepdims=True)


def with_square(both, square, core):
    lane = lax.broadcasted_iota(jnp.int32, (16, 128), 1)
    high = square.astype(BF16).astype(F32)
    terms = jnp.concatenate([high, square - high], axis=0)
    first = jnp.where((core == 1) & (lane < 64), terms, both[:, 0:128])
    last = jnp.where((core == 0) & (lane >= 64), terms, both[:, 384:512])
    return jnp.concatenate([first, both[:, 128:384], last], axis=1)


def square_of(both, core):
    lane = lax.broadcasted_iota(jnp.int32, (16, 128), 1)
    tile = jnp.where(core == 1, both[:, 0:128], pltpu.roll(both[:, 384:512], 64, 1))
    tile = jnp.where(lane < 64, tile, pltpu.roll(tile, 64, 1))
    return tile[0:8] + tile[8:16]


def merged(ref):
    lines = ref[pl.ds(8, 16, stride=16), :]
    head = lax.broadcasted_iota(jnp.int32, (16, 128), 1) < 8
    peak = jnp.max(lines, axis=0, keepdims=True)
    factors = jnp.where(head, jnp.exp(jnp.where(head, lines - peak, 0.0)), 0.0)
    total = jnp.sum(factors * pltpu.roll(lines, 120, 1), axis=0, keepdims=True)
    terms = [column_of(factors[i : i + 1]) * ref[i * 16 : i * 16 + 8, :] for i in range(16)]
    while len(terms) > 1:
        terms = [a + b for a, b in zip(terms[0::2], terms[1::2])]
    return column_of(peak), column_of(total), terms[0]


def kernel(
    h_lengths, h_tokens, h_attn_gain, h_ffn_gain, h_freq,
    h_q, h_k, h_v, h_o, h_gate, h_up, h_down, h_kc, h_vc,
    out_ref,
    lengths, tokens, attn_gain, ffn_gain, freq,
    w_q, w_k, w_v, w_o, w_gate, w_up, w_down, k_c, v_c,
    s_qkv, r_qkv, r_qkv2,
    s_att, r_att, r_attn,
    r_out,
    s_ffn, r_ffn, r_ffn2, r_hid,
    r_down,
    load_sem, send_sem, recv_sem, near_sem,
):
    ctx = lax.axis_index("ctx")
    kvh = lax.axis_index("kvh")
    xc = lax.rem(ctx, 8)
    z = ctx // 8
    x = xc // 2
    c = lax.rem(xc, 2)

    def xc_peer(step):
        dx, dc = step
        to = lax.rem(x + dx, 4) * 2 + lax.rem(c + dc, 2)
        return to, (z * 8 + to, kvh)

    def z_peer(d):
        return (lax.rem(z + d, 8) * 8 + xc, kvh)

    def z_other(d):
        return (lax.rem(z + d, 8) * 8 + x * 2 + (1 - c), kvh)

    def y_peer(d):
        return (ctx, lax.rem(kvh + d, 8))

    def zc_peers():
        for d in FAR_FIRST:
            yield c, (lax.rem(z + d, 8) * 8 + xc, kvh)
            yield 1 - c, (lax.rem(z + d, 8) * 8 + x * 2 + (1 - c), kvh)
        yield 1 - c, (z * 8 + x * 2 + (1 - c), kvh)

    def send(src, dst, stage, peer):
        pltpu.make_async_remote_copy(
            src_ref=src, dst_ref=dst, send_sem=send_sem.at[stage], recv_sem=recv_sem.at[stage],
            device_id=peer, device_id_type=MESH,
        ).start()

    def arrived(ref, stage):
        pltpu.make_async_copy(ref, ref, recv_sem.at[stage]).wait()

    barrier = pltpu.get_barrier_semaphore()
    near = [z_peer(d) for d in (2, 6, 1, 7)] + [z_other(d) for d in (2, 6, 1, 7)] + [y_peer(1), y_peer(7)]
    for peer in near + [xc_peer(d)[1] for d in RING]:
        pl.semaphore_signal(barrier, inc=1, device_id=peer, device_id_type=MESH)

    def tell(i, peer_at, steps=(1, 7)):
        for d in steps:
            pl.semaphore_signal(near_sem.at[i], inc=1, device_id=peer_at(d), device_id_type=MESH)

    def heard(i, count=2):
        pl.semaphore_wait(near_sem.at[i], count)

    loads = {}
    for i, (name, src, dst) in enumerate(
        (
            ("tokens", h_tokens, tokens), ("attn_gain", h_attn_gain, attn_gain),
            ("q", h_q, w_q), ("k", h_k, w_k), ("v", h_v, w_v),
            ("lengths", h_lengths, lengths), ("freq", h_freq, freq), ("ffn_gain", h_ffn_gain, ffn_gain),
            ("kc", h_kc.at[x], k_c.at[x]), ("vc", h_vc.at[x], v_c.at[x]),
            ("o", h_o, w_o), ("gate", h_gate, w_gate), ("up", h_up, w_up), ("down", h_down, w_down),
        )
    ):
        loads[name] = pltpu.make_async_copy(src, dst, load_sem.at[i])
        loads[name].start()
    loads["tokens"].wait()
    loads["attn_gain"].wait()
    hid = jnp.concatenate([tokens[0], tokens[1]], axis=0).astype(F32)
    sq = jnp.broadcast_to(jnp.sum(hid * hid, axis=1, keepdims=True), (8, 128))
    xg = (hid * attn_gain[...].astype(F32)).astype(BF16)
    for name in ("q", "k", "v"):
        loads[name].wait()
    q_part = jnp.dot(xg, w_q[...], preferred_element_type=F32)
    k_part = jnp.dot(xg, w_k[...], preferred_element_type=F32)
    v_part = jnp.dot(xg, w_v[...], preferred_element_type=F32)
    for h in range(8):
        s_qkv[pl.ds(h, 8, stride=16), :] = q_part[:, h * 128 : (h + 1) * 128]
    s_qkv[pl.ds(8, 8, stride=16), :] = k_part
    s_qkv[pl.ds(9, 8, stride=16), :] = v_part
    s_qkv[pl.ds(10, 8, stride=16), :] = sq

    def row_block(to):
        return pl.ds(pl.multiple_of((lax.rem(to, 2) * 4 + to // 2) * 16, 16), 11)

    r_qkv[xc, 0:11, :] = s_qkv[row_block(xc), :]

    pl.semaphore_wait(barrier, 17)
    tell(0, z_peer, (2, 6, 1, 7))
    for d in RING:
        to, peer = xc_peer(d)
        send(s_qkv.at[row_block(to)], r_qkv.at[xc, pl.ds(0, 11)], QKV_RS, peer)
    for d in (2, 1, 3):
        to = lax.rem(x + d, 4)
        peer = (z * 8 + to * 2 + c, kvh)
        send(h_kc.at[to], k_c.at[x], K_MOVE, peer)

    for d in (2, 1, 3):
        to = lax.rem(x + d, 4)
        send(h_vc.at[to], v_c.at[x], V_MOVE, (z * 8 + to * 2 + c, kvh))
    heard(0, 4)

    loads["lengths"].wait()
    loads["freq"].wait()
    step8 = lax.broadcasted_iota(jnp.int32, (8, 128), 0)
    lane = lax.broadcasted_iota(jnp.int32, (8, 128), 1)
    length = lengths[x]
    angle = (length + step8).astype(F32) * freq[...]
    cosine = jnp.cos(angle)
    sine = jnp.sin(angle)
    sine = jnp.where(lane < 64, -sine, sine)

    tell(3, y_peer)
    arrived(r_qkv.at[pl.ds(0, 7), pl.ds(0, 11)], QKV_RS)
    r_qkv2[z * 2 + c, 0:11, :] = total_of(r_qkv, pl.ds(0, 11))
    mine = r_qkv2.at[z * 2 + c, pl.ds(0, 11)]
    for _, peer in zc_peers():
        send(mine, mine, QKV_AR, peer)
    heard(3)
    tell(4, y_peer)
    arrived(r_qkv2.at[pl.ds(0, 15), pl.ds(0, 11)], QKV_AR)
    queries, new_keys, new_values = [], [], []
    for s in range(2):
        parts = [r_qkv2[i * 2 + s, 0:11, :] for i in range(8)]
        while len(parts) > 1:
            parts = [a + b for a, b in zip(parts[0::2], parts[1::2])]
        whole = parts[0]
        scale = lax.rsqrt(whole[10:11] / D + EPS)

        def rotary(a):
            return a * cosine[s : s + 1] + pltpu.roll(a, 64, 1) * sine[s : s + 1]

        queries.append(rotary(whole[0:8] * scale).astype(BF16))
        key = jnp.broadcast_to(whole[8:9] * scale, (8, 128))
        new_keys.append(rotary(key).astype(BF16).astype(F32))
        value = jnp.broadcast_to(whole[9:10] * scale, (8, 128))
        new_values.append(value.astype(BF16).astype(F32))
    both_steps = jnp.concatenate(queries, axis=0)
    loads["kc"].wait()
    loads["vc"].wait()
    arrived(k_c.at[pl.ds(0, 3)], K_MOVE)

    scores, valid = [], []
    for i in range(4):
        scores.append(
            lax.dot_general(both_steps, k_c[i], (((1,), (1,)), ((), ())), preferred_element_type=F32)
            / math.sqrt(128)
        )
        first = (z * 8 + i * 2 + c) * 256
        valid.append(first + lax.broadcasted_iota(jnp.int32, (16, 256), 1) < length)
    scores = jnp.concatenate(scores, axis=1)
    valid = jnp.concatenate(valid, axis=1)
    scores = jnp.where(valid, scores, -1e30)
    peak = jnp.max(scores, axis=1, keepdims=True)
    weights = jnp.where(valid, jnp.exp(scores - peak), 0.0)
    total = jnp.sum(weights, axis=1, keepdims=True)
    weights = weights.astype(BF16)
    arrived(v_c.at[pl.ds(0, 3)], V_MOVE)
    acc = jnp.zeros((16, 128), F32)
    for i in range(4):
        acc += jnp.dot(weights[:, i * 256 : (i + 1) * 256], v_c[i], preferred_element_type=F32)
    for s in range(2):
        rows = slice(s * 8, s * 8 + 8)
        s_att[s, 0:8, :] = acc[rows]
        line = jnp.where(lane == step8, peak[rows], jnp.where(lane == step8 + 8, total[rows], 0.0))
        s_att[s, 8:9, :] = jnp.sum(line, axis=0, keepdims=True)
    slot = pl.ds(pl.multiple_of((z * 2 + c) * 16, 16), 9)
    r_att[slot, :] = s_att[c, 0:9, :]
    for core, peer in zc_peers():
        send(s_att.at[core, pl.ds(0, 9)], r_att.at[slot], ATT_AR, peer)

    q_mine = jnp.where(c == 0, queries[0].astype(F32), queries[1].astype(F32))
    fresh = [jnp.sum(q_mine * key, axis=1, keepdims=True) / math.sqrt(128) for key in new_keys]
    f_first = jnp.broadcast_to(fresh[0], (8, 128))
    f_second = jnp.where(c == 1, jnp.broadcast_to(fresh[1], (8, 128)), -1e30)

    heard(4)
    tell(5, y_peer)
    heard(5)
    loads["o"].wait()
    arrived(r_att.at[pl.ds(0, 15 * 9)], ATT_AR)
    peak, total, summed = merged(r_att)
    top = jnp.maximum(peak, jnp.maximum(f_first, f_second))
    factor = jnp.exp(peak - top)
    e_first = jnp.exp(f_first - top)
    e_second = jnp.where(c == 1, jnp.exp(f_second - top), 0.0)
    total = total * factor + e_first + e_second
    summed = (
        summed * factor
        + e_first.astype(BF16).astype(F32) * new_values[0]
        + e_second.astype(BF16).astype(F32) * new_values[1]
    )
    mine = r_attn.at[pl.ds(pl.multiple_of((c * 4 + x) * 8, 8), 8)]
    mine[...] = summed / total
    for d in RING:
        send(mine, mine, ATT_AG, xc_peer(d)[1])
    arrived(r_attn.at[pl.ds(0, 56)], ATT_AG)

    attn = jnp.concatenate([r_attn[pl.ds(h, 8, stride=8), :] for h in range(8)], axis=1).astype(BF16)
    r_out[kvh] = jnp.dot(attn, w_o[...], preferred_element_type=F32)
    for d in FAR_FIRST:
        send(r_out.at[kvh], r_out.at[kvh], OUT_AR, y_peer(d))
    for name in ("gate", "up", "ffn_gain"):
        loads[name].wait()
    arrived(r_out.at[pl.ds(0, 7)], OUT_AR)
    attended = total_of(r_out, pl.ds(0, 8))
    x_mid = hid + attended
    square = jnp.broadcast_to(jnp.sum(x_mid * x_mid, axis=1, keepdims=True), (8, 128))

    xh = (x_mid * ffn_gain[...].astype(F32)).astype(BF16)
    for d in RING + ((0, 0),):
        to, peer = xc_peer(d)
        start = pl.multiple_of(((to // 2) * 7 + lax.rem(to, 2) * 3) * 128, 128)
        gate = jnp.dot(xh, w_gate[:, pl.ds(start, BLOCK)], preferred_element_type=F32)
        up = jnp.dot(xh, w_up[:, pl.ds(start, BLOCK)], preferred_element_type=F32)
        both = with_square(jnp.concatenate([gate, up], axis=0), square, lax.rem(to, 2)).astype(BF16)
        if d != (0, 0):
            s_ffn[to] = both
            send(s_ffn.at[to], r_ffn.at[xc], FFN_RS, peer)
        else:
            r_ffn[xc] = both
    out_ref[0] = attended[0:4].astype(BF16)
    out_ref[1] = attended[4:8].astype(BF16)
    arrived(r_ffn.at[pl.ds(0, 7)], FFN_RS)
    both = total_of(r_ffn, pl.ds(0, 16))
    r_ffn2[z] = with_square(both, square_of(both, c), c).astype(BF16)
    for d in FAR_FIRST:
        send(r_ffn2.at[z], r_ffn2.at[z], FFN_AR, z_peer(d))
    loads["down"].wait()
    arrived(r_ffn2.at[pl.ds(0, 7)], FFN_AR)
    both = total_of(r_ffn2, pl.ds(0, 16))
    scale = lax.rsqrt(square_of(both, c) / D + EPS)[:, 0:1]
    gate = both[0:8] * scale
    hidden = gate / (1.0 + jnp.exp(-gate)) * (both[8:16] * scale)
    unit = lax.broadcasted_iota(jnp.int32, (8, BLOCK), 1)
    hidden = jnp.where((unit >= c * 64) & (unit < 448 + c * 64), hidden, 0.0)
    r_hid[xc] = jnp.concatenate([hidden[:, 0:256], hidden[:, 256:512]], axis=0).astype(BF16)
    for d in RING:
        send(r_hid.at[xc], r_hid.at[xc], FFN_AG, xc_peer(d)[1])
    arrived(r_hid.at[pl.ds(0, 7)], FFN_AG)

    pieces = []
    for j in range(4):
        even = r_hid[2 * j].astype(F32)
        odd = r_hid[2 * j + 1].astype(F32)
        pieces += [
            even[0:8], even[8:16, 0:128], even[8:16, 128:256] + odd[0:8, 0:128], odd[0:8, 128:256], odd[8:16]
        ]
    r_down[kvh] = jnp.dot(
        jnp.concatenate(pieces, axis=1).astype(BF16), w_down[...], preferred_element_type=F32
    )
    for d in FAR_FIRST:
        send(r_down.at[kvh], r_down.at[kvh], DOWN_AR, y_peer(d))
    sent = (
        (r_qkv.at[pl.ds(0, 7), pl.ds(0, 11)], (QKV_RS,)),
        (r_qkv2.at[pl.ds(0, 15), pl.ds(0, 11)], (QKV_AR,)),
        (k_c.at[pl.ds(0, 3)], (K_MOVE, V_MOVE)),
        (r_att.at[pl.ds(0, 15 * 9)], (ATT_AR,)),
        (r_attn.at[pl.ds(0, 56)], (ATT_AG,)),
        (r_out.at[pl.ds(0, 7)], (OUT_AR,)),
        (r_ffn.at[pl.ds(0, 7)], (FFN_RS, FFN_AR)),
        (r_hid.at[pl.ds(0, 7)], (FFN_AG,)),
        (r_down.at[pl.ds(0, 7)], (DOWN_AR,)),
    )
    for ref, stages in sent:
        for stage in stages:
            pltpu.make_async_copy(ref, ref, send_sem.at[stage]).wait()
    arrived(r_down.at[pl.ds(0, 7)], DOWN_AR)
    layer = x_mid + total_of(r_down, pl.ds(0, 8))
    out_ref[2] = layer[0:4].astype(BF16)
    out_ref[3] = layer[4:8].astype(BF16)


def body(tokens, lengths, attn_gain, ffn_gain, w_q, w_k, w_v, w_o, w_gate, w_up, w_down, k_cache, v_cache):
    half = np.arange(64, dtype=np.float64)
    freq = np.tile(500000.0 ** (-2.0 * half / 128.0), 2).astype(np.float32)[None]
    k_cache = k_cache.reshape(4, 256, 128)
    v_cache = v_cache.reshape(4, 256, 128)
    hbm = pl.BlockSpec(memory_space=pltpu.HBM)
    small = (tokens, attn_gain.reshape(1, 128), ffn_gain.reshape(1, 128), jnp.asarray(freq))
    weights = (w_q, w_k, w_v, w_o, w_gate, w_up, w_down, k_cache, v_cache)
    both = pl.pallas_call(
        kernel,
        out_shape=pltpu.VMEM((4, 4, 128), BF16),
        in_specs=[hbm] * 14,
        out_specs=pl.BlockSpec(memory_space=pltpu.VMEM),
        scratch_shapes=[pltpu.SMEM((4,), jnp.int32)]
        + [pltpu.VMEM(a.shape, a.dtype) for a in small + weights]
        + [
            pltpu.VMEM((144, 128), F32), pltpu.VMEM((8, 16, 128), F32), pltpu.VMEM((16, 16, 128), F32),
            pltpu.VMEM((2, 16, 128), F32), pltpu.VMEM((272, 128), F32),
            pltpu.VMEM((72, 128), F32),
            pltpu.VMEM((8, 8, 128), F32),
            pltpu.VMEM((8, 16, BLOCK), BF16), pltpu.VMEM((8, 16, BLOCK), BF16), pltpu.VMEM((8, 16, BLOCK), BF16),
            pltpu.VMEM((8, 16, 256), BF16),
            pltpu.VMEM((8, 8, 128), F32),
            pltpu.SemaphoreType.DMA((14,)),
            pltpu.SemaphoreType.DMA((11,)),
            pltpu.SemaphoreType.DMA((11,)),
            pltpu.SemaphoreType.REGULAR((6,)),
        ],
        compiler_params=pltpu.CompilerParams(
            collective_id=0, has_side_effects=True, vmem_limit_bytes=60 * 1024 * 1024
        ),
    )(*[pltpu.with_memory_space_constraint(a, pltpu.HBM) for a in (lengths, *small, *weights)])
    return both[0:2], both[2:4]


def solution(mesh):
    return jax.shard_map(
        body,
        mesh=mesh,
        in_specs=(
            P(None, None, "ctx"),
            P(),
            P("ctx"),
            P("ctx"),
            P("ctx", "kvh"),
            P("ctx", "kvh"),
            P("ctx", "kvh"),
            P("kvh", "ctx"),
            P("ctx", "kvh"),
            P("ctx", "kvh"),
            P("kvh", "ctx"),
            P(None, "ctx", "kvh", None),
            P(None, "ctx", "kvh", None),
        ),
        out_specs=(P(None, None, "ctx"), P(None, None, "ctx")),
        check_vma=False,
    )
```
